32 devices in a mesh: pb: 4 (over y, x), kv: 4 (over z), ha: 2 (over core).
Axes of the slice: x: 2, y: 2, z: 4, core: 2. Of those that a mesh axis runs over, the one named last changes fastest.
Arguments:
- teacher_q: bfloat16 [2048, 4096], P(('pb', 'kv'), 'ha'), may hold values from -240 to 240
- teacher_k: bfloat16 [2048, 1024], P(('pb', 'kv'), 'ha'), may hold values from -6 to 6
- teacher_v: bfloat16 [2048, 1024], P(('pb', 'kv'), 'ha'), may hold values from -6 to 6
- student_q: bfloat16 [2048, 2048], P(('pb', 'kv'), 'ha'), may hold values from -240 to 240
- student_k: bfloat16 [2048, 512], P(('pb', 'kv'), 'ha'), may hold values from -6 to 6
- student_v: bfloat16 [2048, 512], P(('pb', 'kv'), 'ha'), may hold values from -6 to 6
- doc_ids: int32 [2048], P(('pb', 'kv')), may hold values from 0 to 3, never falling along the last dimension, each value on 1 to 1536 neighbouring positions
- proj_weight: bfloat16 [32, 64, 128], replicated, may hold values from -0.75 to 0.75
Outputs:
- grad_w: float32 [2048, 128], P(('pb', 'kv', 'ha'))
- token_loss: float32 [2048], P(('pb', 'kv', 'ha'))
The draws below stay inside these ranges and needn't reach their ends.
Inputs may be any that keep to these rules, and one draw needn't show every extreme that they name: `doc_ids`: document numbers never fall along the sequence; each document spans 1 to 1536 tokens, and one spans exactly that many.
All inputs are finite; a program needn't handle non-finite values.
Results may differ from the reference program's by a relative error of at most 0.0035.
Values may be sent and summed in bfloat16 or wider, within the bound.
A program may use at most 128 MiB of HBM per device.

```python
import math
import jax
import jax.numpy as jnp
import numpy as np
from jax import lax

QH = 32
KVH = 8
TD = 128
SD = 64
DOCS = 4
TOKENS = 2048


def paired_draw(key, salt, head_size):
    key = jax.random.fold_in(key, salt)
    key_key, query_key = jax.random.split(key, 2)
    per_group = QH // KVH
    keys_raw = jnp.clip(jax.random.normal(key_key, (TOKENS, KVH, head_size), jnp.float32), -6.0, 6.0)
    queries_raw = jnp.clip(jax.random.normal(query_key, (TOKENS, KVH, per_group, head_size), jnp.float32), -6.0, 6.0)
    keys_final = keys_raw
    queries_final = queries_raw
    queries_final = jnp.clip(queries_final, -240.0, 240.0)
    return (queries_final.reshape(TOKENS, QH * head_size), keys_final.reshape(TOKENS, KVH * head_size))


def draw_teacher_q(key, part):
    return paired_draw(key, 5, TD)[0].astype(jnp.bfloat16)


def draw_teacher_k(key, part):
    return paired_draw(key, 5, TD)[1].astype(jnp.bfloat16)


def draw_student_q(key, part):
    return paired_draw(key, 7, SD)[0].astype(jnp.bfloat16)


def draw_student_k(key, part):
    return paired_draw(key, 7, SD)[1].astype(jnp.bfloat16)


def block_levels(rng, extent, pieces, least, top_value):
    level = 1.0
    for axis_at, parts in pieces:
        draws = jax.random.uniform(jax.random.fold_in(jax.random.fold_in(rng, 6), axis_at), (parts,), jnp.float32, least / len(pieces), top_value / len(pieces))
        level = level * jnp.repeat(jnp.exp(draws), extent[axis_at] // parts).reshape((-1,) + (1,) * (len(extent) - 1 - axis_at))
    return level


def profile(amount, total, reach, lean):
    loads = [(1 << 20) // math.isqrt(grade ** lean) + 1 for grade in range(2, amount + 1)]
    surplus, counts = total - reach - (amount - 1), [1] * (amount - 1)
    while surplus > 0:
        free = [i for i in range(amount - 1) if counts[i] < reach]
        pool, budget = sum([loads[i] for i in free]), surplus
        for i in free:
            extra = min(reach - counts[i], max(1, budget * loads[i] // pool), surplus)
            counts[i] = counts[i] + extra
            surplus = surplus - extra
    return np.array([reach] + counts)


def ragged(stream_key, count, total, limit, skew):
    if count == 2:
        one = jax.random.randint(stream_key, (), max(1, total - limit), min(limit, total - 1) + 1)
        return jnp.stack([one, total - one])
    tallies = jnp.asarray(profile(count, total, limit, skew), jnp.int32)
    pairs = (count - 1) // 2
    source_of, taker = tallies[1:1 + 2 * pairs:2], tallies[2:2 + 2 * pairs:2]
    margin = jnp.minimum(source_of - 1, limit - taker)
    shifted = jax.random.randint(jax.random.fold_in(stream_key, 1), (pairs,), 0, 1 << 20) % (margin + 1)
    tallies = tallies.at[1:1 + 2 * pairs:2].set(source_of - shifted).at[2:2 + 2 * pairs:2].set(taker + shifted)
    return tallies[jax.random.permutation(jax.random.fold_in(stream_key, 2), count)]


def noise(own_key, dims, width, most, cuts=(), held_as=jnp.bfloat16):
    drawn = jax.random.normal(own_key, dims, jnp.float32) * width
    if len(cuts) > 0:
        drawn = block_levels(own_key, dims, cuts, -0.22, 0.18) * drawn
    return jnp.clip(drawn, min=-most, max=most).astype(held_as)


def setup_inputs(seed: int = 0) -> dict:
    key_list = jax.random.split(jax.random.key(seed), 9)
    teacher_q = draw_teacher_q(jax.random.fold_in(key_list[8], 71), 0)
    teacher_k = draw_teacher_k(jax.random.fold_in(key_list[8], 71), 0)
    teacher_v = noise(key_list[2], (TOKENS, KVH * TD), 1.0, 6.0, ((0, 16), (1, 2)))
    student_q = draw_student_q(jax.random.fold_in(key_list[8], 71), 0)
    student_k = draw_student_k(jax.random.fold_in(key_list[8], 71), 0)
    student_v = noise(key_list[5], (TOKENS, KVH * SD), 1.0, 6.0, ((0, 16), (1, 2)))
    doc_ids = jnp.searchsorted(jnp.cumsum(ragged(key_list[6], DOCS, TOKENS, 3 * TOKENS // 4, 1)), jnp.arange(TOKENS), side="right").astype(jnp.int32)
    proj_weight = noise(key_list[7], (QH, SD, TD), SD ** -0.5, 0.75)
    return {"teacher_q": teacher_q, "teacher_k": teacher_k, "teacher_v": teacher_v, "student_q": student_q, "student_k": student_k, "student_v": student_v, "doc_ids": doc_ids, "proj_weight": proj_weight}


NEGATIVE = -1e+30
EPSILON = 1e-06

def model_attention(queries, keys_all, values_all, doc_ids, head_size):
    total = queries.shape[0]
    groups = keys_all.shape[1] // head_size
    per_group = queries.shape[1] // (groups * head_size)
    block = math.gcd(total, 256)
    scale = 1.0 / math.sqrt(head_size)
    keyed = keys_all.reshape(total, groups, head_size).astype(jnp.float32)
    valued = values_all.reshape(total, groups, head_size).astype(jnp.float32)
    positions = jnp.arange(total, dtype=jnp.int32)
    query_blocks = queries.reshape(total // block, block, groups, per_group, head_size)
    position_blocks = positions.reshape(total // block, block)
    doc_blocks = doc_ids.reshape(total // block, block)

    def one_block(item):
        query_block, position_block, doc_block = item
        scores = jnp.einsum('qgpd,kgd->gpqk', query_block.astype(jnp.float32), keyed) * scale
        allowed = (doc_block[:, None] == doc_ids[None, :]) & (positions[None, :] <= position_block[:, None])
        scores = jnp.where(allowed, scores, NEGATIVE)
        largest = lax.optimization_barrier(jnp.max(scores, axis=-1, keepdims=True))
        weights = jnp.where(allowed, jnp.exp(scores - largest), 0.0)
        totals = lax.optimization_barrier(jnp.sum(weights, axis=-1))
        rounded = lax.optimization_barrier(weights.astype(jnp.bfloat16)).astype(jnp.float32)
        mixed = jnp.einsum('gpqk,kgd->gpqd', rounded, valued) / totals[..., None]
        return jnp.transpose(mixed, (2, 0, 1, 3)).reshape(block, groups * per_group * head_size)
    outputs = lax.map(one_block, (query_blocks, position_blocks, doc_blocks))
    return outputs.reshape(total, -1).astype(jnp.bfloat16)

def distill(teacher_out, student_out, proj_weight, total_tokens):
    count = teacher_out.shape[0]
    heads = proj_weight.shape[0]
    teacher_float = teacher_out.astype(jnp.float32)
    target = teacher_float * lax.rsqrt(lax.optimization_barrier(jnp.mean(teacher_float * teacher_float, axis=1, keepdims=True)) + EPSILON)
    student_float = student_out.astype(jnp.float32)
    features = (student_float * lax.rsqrt(lax.optimization_barrier(jnp.mean(student_float * student_float, axis=1, keepdims=True)) + EPSILON)).astype(jnp.bfloat16)
    feature_heads = features.reshape(count, heads, -1).astype(jnp.float32)
    predicted = jnp.einsum('thd,hde->the', feature_heads, proj_weight.astype(jnp.float32), precision=lax.Precision.HIGHEST)
    difference = predicted.reshape(count, -1) - target
    token_loss = lax.optimization_barrier(jnp.mean(difference * difference, axis=1))
    gradient = jnp.einsum('thd,the->hde', feature_heads, difference.reshape(count, heads, -1), precision=lax.Precision.HIGHEST)
    gradient = gradient / math.sqrt(total_tokens)
    return (gradient.reshape(-1, gradient.shape[2]), token_loss)

def reference(teacher_q, teacher_k, teacher_v, student_q, student_k, student_v, doc_ids, proj_weight):
    teacher_out = model_attention(teacher_q, teacher_k, teacher_v, doc_ids, TD)
    student_out = model_attention(student_q, student_k, student_v, doc_ids, SD)
    grad_w, token_loss = distill(teacher_out, student_out, proj_weight, TOKENS)
    return (grad_w, token_loss)
```

```python
import functools
import math

import jax
import jax.numpy as jnp
from jax import lax
from jax.experimental import pallas as pl
from jax.experimental.pallas import tpu as pltpu
from jax.sharding import PartitionSpec as P

MESH = pl.DeviceIdType.MESH

TD = 128
SD = 64
DOCS = 4


NEGATIVE = -1e30
EPSILON = 1e-06


def start_state(queries, head_size, groups):
    queried = queries.shape[0]
    per_group = queries.shape[1] // (groups * head_size)
    largest = jnp.full((groups, per_group, queried), NEGATIVE, jnp.float32)
    totals = jnp.zeros((groups, per_group, queried), jnp.float32)
    accum = jnp.zeros((groups, per_group, queried, head_size), jnp.float32)
    return (largest, totals, accum)


def attend_keys(
    state, queries, query_pos, query_doc, keys_piece, values_piece, key_pos, key_doc, head_size
):
    length = keys_piece.shape[0]
    block = math.gcd(length, 512)
    blocks = length // block
    groups = keys_piece.shape[1] // head_size
    queried = queries.shape[0]
    per_group = queries.shape[1] // (groups * head_size)
    shaped = queries.reshape(queried, groups, per_group, head_size)
    scale = 1.0 / math.sqrt(head_size)
    newest = jnp.max(query_pos)

    def compute(current, key_block, value_block, pos_block, doc_block):
        largest, totals, accum = current
        scores = (
            jnp.einsum(
                "qgpd,kgd->gpqk",
                shaped,
                key_block.reshape(block, groups, head_size),
                preferred_element_type=jnp.float32,
            )
            * scale
        )
        allowed = (query_doc[:, None] == doc_block[None, :]) & (
            pos_block[None, :] <= query_pos[:, None]
        )
        scores = jnp.where(allowed, scores, NEGATIVE)
        updated = jnp.maximum(largest, jnp.max(scores, axis=-1))
        weights = jnp.where(allowed, jnp.exp(scores - updated[..., None]), 0.0)
        factor = jnp.exp(largest - updated)
        totals = totals * factor + jnp.sum(weights, axis=-1)
        mixed = jnp.einsum(
            "gpqk,kgd->gpqd",
            weights.astype(jnp.bfloat16),
            value_block.reshape(block, groups, head_size),
            preferred_element_type=jnp.float32,
        )
        return (updated, totals, accum * factor[..., None] + mixed)

    def visit(current, item):
        key_block, value_block, pos_block, doc_block = item
        result = lax.cond(
            pos_block[0] <= newest,
            lambda inner: compute(inner, key_block, value_block, pos_block, doc_block),
            lambda inner: inner,
            current,
        )
        return (result, None)

    items = (
        keys_piece.reshape(blocks, block, -1),
        values_piece.reshape(blocks, block, -1),
        key_pos.reshape(blocks, block),
        key_doc.reshape(blocks, block),
    )
    final, unused = lax.scan(visit, state, items)
    return final


def finish(totals, accum):
    queried = accum.shape[2]
    result = accum / totals[..., None]
    return jnp.transpose(result, (2, 0, 1, 3)).reshape(queried, -1).astype(jnp.bfloat16)


def gathered(teacher_q, teacher_k, teacher_v, student_q, student_k, student_v, doc_ids, proj_weight):
    shard_rows = teacher_q.shape[0]
    groups = teacher_k.shape[1] // TD
    outer = lax.axis_size("pb")
    inner_size = lax.axis_size("kv")
    total_tokens = shard_rows * outer * inner_size
    shard = lax.axis_index("pb") * inner_size + lax.axis_index("kv")
    own_pos = shard * shard_rows + jnp.arange(shard_rows, dtype=jnp.int32)
    initial = (start_state(teacher_q, TD, groups), start_state(student_q, SD, groups))
    key_teacher = lax.all_gather(teacher_k, ("pb", "kv"), axis=0, tiled=True)
    value_teacher = lax.all_gather(teacher_v, ("pb", "kv"), axis=0, tiled=True)
    key_student = lax.all_gather(student_k, ("pb", "kv"), axis=0, tiled=True)
    value_student = lax.all_gather(student_v, ("pb", "kv"), axis=0, tiled=True)
    piece_doc = lax.all_gather(doc_ids, ("pb", "kv"), axis=0, tiled=True)
    key_pos = jnp.arange(piece_doc.shape[0], dtype=jnp.int32)
    teacher_state = attend_keys(
        initial[0], teacher_q, own_pos, doc_ids, key_teacher, value_teacher, key_pos, piece_doc, TD
    )
    student_state = attend_keys(
        initial[1], student_q, own_pos, doc_ids, key_student, value_student, key_pos, piece_doc, SD
    )
    teacher_state, student_state = (teacher_state, student_state)
    teacher_out = finish(teacher_state[1], teacher_state[2])
    student_out = finish(student_state[1], student_state[2])
    teacher_half, student_half = (
        lax.all_to_all(teacher_out, "ha", split_axis=0, concat_axis=1, tiled=True),
        lax.all_to_all(student_out, "ha", split_axis=0, concat_axis=1, tiled=True),
    )
    count = teacher_half.shape[0]
    heads = proj_weight.shape[0]
    teacher_float = teacher_half.astype(jnp.float32)
    target = teacher_float * lax.rsqrt(
        jnp.mean(teacher_float * teacher_float, axis=1, keepdims=True) + EPSILON
    )
    student_float = student_half.astype(jnp.float32)
    features = (
        student_float
        * lax.rsqrt(jnp.mean(student_float * student_float, axis=1, keepdims=True) + EPSILON)
    ).astype(jnp.bfloat16)
    feature_heads = features.reshape(count, heads, -1)
    predicted = jnp.einsum(
        "thd,hde->the", feature_heads, proj_weight, preferred_element_type=jnp.float32
    )
    difference = predicted.reshape(count, -1) - target
    token_loss = jnp.mean(difference * difference, axis=1)
    gradient = jnp.einsum(
        "thd,the->hde",
        feature_heads.astype(jnp.float32),
        difference.reshape(count, heads, -1),
        precision=lax.Precision.HIGHEST,
    )
    gradient = (gradient / math.sqrt(total_tokens)).reshape(-1, gradient.shape[2])
    grad_w = lax.psum_scatter(gradient, ("pb", "kv", "ha"), scatter_dimension=0, tiled=True)
    return (grad_w, token_loss)

def rows_dot(a, b):
    return lax.dot_general(a, b, (((1,), (1,)), ((), ())), preferred_element_type=jnp.float32)


def columns_dot(a, b):
    return lax.dot_general(a, b, (((0,), (0,)), ((), ())), preferred_element_type=jnp.float32)


def fused(
    shape,
    tokens,
    tq_ref,
    tk_ref,
    tv_ref,
    sq_ref,
    sk_ref,
    sv_ref,
    doc_ref,
    w_ref,
    grad_ref,
    loss_ref,
    stage,
    kv,
    tq_in,
    sq_in,
    tq_all,
    sq_all,
    t_acc,
    s_acc,
    soft,
    stats,
    losses,
    grads,
    grads_in,
    xy_send,
    xy_recv,
    q_send,
    q_recv,
    up_send,
    up_recv,
    down_send,
    down_recv,
    stat_send,
    stat_recv,
    loss_send,
    loss_recv,
    grad_send,
    grad_recv,
):
    npb, nkv, nha = shape
    devices = npb * nkv * nha
    rows = tq_ref.shape[0]
    heads = tq_ref.shape[1] // (npb * TD)
    wide = heads * rows
    pb, z, ha = lax.axis_index("pb"), lax.axis_index("kv"), lax.axis_index("ha")
    me = (pb * nkv + z) * nha + ha

    def coords(index):
        return (index // (nkv * nha), (index // nha) % nkv, index % nha)

    barrier = pltpu.get_barrier_semaphore()

    def greet(r, carry):
        pl.semaphore_signal(
            barrier, inc=1, device_id=coords((me + r) % devices), device_id_type=MESH
        )
        return carry

    lax.fori_loop(1, devices, greet, 0)

    doc_rows = jnp.broadcast_to(doc_ref[...].astype(jnp.float32), (16, rows)).astype(jnp.bfloat16)
    for g in range(npb):
        stage[g, 0:rows, :] = tk_ref[:, g * TD : (g + 1) * TD]
        stage[g, rows : 2 * rows, :] = tv_ref[:, g * TD : (g + 1) * TD]
        stage[g, 2 * rows : 3 * rows, :] = jnp.concatenate(
            [sk_ref[:, g * SD : (g + 1) * SD], sv_ref[:, g * SD : (g + 1) * SD]], axis=1
        )
        stage[g, 3 * rows : 3 * rows + 16, :] = doc_rows
    kv[z, pb] = stage[pb]

    pl.semaphore_wait(barrier, devices - 1)

    def partner(r):
        return ((pb // 2 + r // 2) % 2) * 2 + (pb % 2 + r % 2) % 2

    def kv_copy(r):
        to = partner(r)
        return pltpu.make_async_remote_copy(
            src_ref=stage.at[to],
            dst_ref=kv.at[z, pb],
            send_sem=xy_send.at[r],
            recv_sem=xy_recv.at[r],
            device_id=(to, z, ha),
            device_id_type=MESH,
        )

    def q_copy(r, which):
        to = partner(r)
        ref, into, width = ((tq_ref, tq_in, heads * TD), (sq_ref, sq_in, heads * SD))[which]
        return pltpu.make_async_remote_copy(
            src_ref=ref.at[:, pl.ds(pl.multiple_of(to * width, width), width)],
            dst_ref=into.at[pb],
            send_sem=q_send.at[r, which],
            recv_sem=q_recv.at[r, which],
            device_id=(to, z, ha),
            device_id_type=MESH,
        )

    for r in range(1, npb):
        kv_copy(r).start()
    for r in range(1, npb):
        q_copy(r, 0).start()
        q_copy(r, 1).start()

    def chain(h, r, up):
        source = z - h if up else z + h
        piece = kv.at[source, partner(r)]
        send, recv = (up_send, up_recv) if up else (down_send, down_recv)
        return pltpu.make_async_remote_copy(
            src_ref=piece,
            dst_ref=piece,
            send_sem=send.at[h, r],
            recv_sem=recv.at[h, r],
            device_id=(pb, z + 1 if up else z - 1, ha),
            device_id_type=MESH,
        )

    def arrived(h, r, up):
        source = z - h if up else z + h
        piece = kv.at[source, partner(r)]
        recv = up_recv if up else down_recv
        send = up_send if up else down_send
        pltpu.make_async_remote_copy(
            src_ref=piece,
            dst_ref=piece,
            send_sem=send.at[h - 1, r],
            recv_sem=recv.at[h - 1, r],
            device_id=(pb, z - 1 if up else z + 1, ha),
            device_id_type=MESH,
        ).wait_recv()

    def first_hop():
        for r in range(npb):
            if r > 0:
                kv_copy(r).wait_recv()

            @pl.when(z < nkv - 1)
            def _():
                chain(0, r, True).start()

            @pl.when(z > 0)
            def _():
                chain(0, r, False).start()

    def next_hop(h):
        for r in range(npb):

            @pl.when(z - h >= 0)
            def _():
                arrived(h, r, True)

                @pl.when(z < nkv - 1)
                def _():
                    chain(h, r, True).start()

            @pl.when(z + h <= nkv - 1)
            def _():
                arrived(h, r, False)

                @pl.when(z > 0)
                def _():
                    chain(h, r, False).start()

    first_hop()
    next_hop(1)

    tq_in[pb] = tq_ref[:, pl.ds(pl.multiple_of(pb * heads * TD, heads * TD), heads * TD)]
    sq_in[pb] = sq_ref[:, pl.ds(pl.multiple_of(pb * heads * SD, heads * SD), heads * SD)]
    for r in range(1, npb):
        q_copy(r, 0).wait_recv()
        q_copy(r, 1).wait_recv()
    blank = jnp.zeros((rows, TD - SD), jnp.bfloat16)
    for p in range(npb):
        for j in range(heads):
            tq_all[p, j * rows : (j + 1) * rows, :] = tq_in[p, :, j * TD : (j + 1) * TD]
            sq_all[p, j * rows : (j + 1) * rows, :] = jnp.concatenate(
                [sq_in[p, :, j * SD : (j + 1) * SD], blank], axis=1
            )
    t_acc[...] = jnp.zeros_like(t_acc)
    s_acc[...] = jnp.zeros_like(s_acc)
    soft[:, 0:2, :] = jnp.full((npb, 2, wide), NEGATIVE, jnp.float32)
    soft[:, 2:4, :] = jnp.zeros((npb, 2, wide), jnp.float32)

    local_key = lax.broadcasted_iota(jnp.int32, (rows, wide), 0)
    local_query = lax.broadcasted_iota(jnp.int32, (1, wide), 1) % rows

    def attend(source):
        firsts = []
        for c in range(npb):
            key_doc = kv[source, c, 3 * rows : 3 * rows + 16, :].astype(jnp.float32)[0:1, :]
            firsts.append(
                [
                    jnp.sum((key_doc < d).astype(jnp.float32), axis=1, keepdims=True)
                    for d in range(1, DOCS)
                ]
            )
        for p in range(npb):
            keys = (p + 1) * rows
            own = kv[z, p, 3 * rows : 3 * rows + 16, :].astype(jnp.float32)[0:1, :]
            query_doc = jnp.concatenate([own] * heads, axis=1)
            allowed = []
            for c in range(p + 1):
                least = jnp.zeros((1, wide), jnp.float32)
                for d in range(1, DOCS):
                    least = jnp.where(query_doc == d, firsts[c][d - 1], least)
                ok = local_key >= least.astype(jnp.int32)
                if c == p:
                    ok = ok & (local_key <= local_query + (z - source) * rows)
                allowed.append(ok)
            for which in range(2):
                size = (TD, SD)[which]
                factor = math.log2(math.e) / math.sqrt(size)
                queries = (tq_all, sq_all)[which][p]
                if which == 0:
                    key_rows = kv[source, 0 : p + 1, 0:rows, :].reshape(keys, TD)
                    value_rows = kv[source, 0 : p + 1, rows : 2 * rows, :].reshape(keys, TD)
                else:
                    key_rows = kv[source, 0 : p + 1, 2 * rows : 3 * rows, :].reshape(keys, TD)
                    value_rows = key_rows
                raw = rows_dot(key_rows, queries) * factor
                scores = jnp.concatenate(
                    [
                        jnp.where(allowed[c], raw[c * rows : (c + 1) * rows], NEGATIVE)
                        for c in range(p + 1)
                    ],
                    axis=0,
                )
                old = soft[p, which : which + 1, :]
                new = jnp.maximum(old, jnp.max(scores, axis=0, keepdims=True))
                weights = jnp.exp2(scores - new)
                shrink = jnp.exp2(old - new)
                soft[p, which : which + 1, :] = new
                soft[p, which + 2 : which + 3, :] = soft[
                    p, which + 2 : which + 3, :
                ] * shrink + jnp.sum(weights, axis=0, keepdims=True)
                mixed = columns_dot(value_rows, weights.astype(jnp.bfloat16))
                if which == 0:
                    t_acc[p] = t_acc[p] * shrink + mixed
                else:
                    s_acc[p] = s_acc[p] * shrink + mixed[TD - SD :]

    def turn(h, carry):
        @pl.when(h >= 2)
        def _():
            next_hop(h)

        below = (z - h >= 0).astype(jnp.int32)
        above = ((z + h <= nkv - 1) & (h > 0)).astype(jnp.int32)

        def visit(i, inner):
            attend(jnp.where((i == 0) & (below == 1), z - h, z + h))
            return inner

        lax.fori_loop(0, below + above, visit, 0)
        return carry

    lax.fori_loop(0, nkv, turn, 0)

    def by_token(row):
        total = row[:, 0:rows]
        for j in range(1, heads):
            total = total + row[:, j * rows : (j + 1) * rows]
        return total

    t_sums, s_sums, t_outs, s_outs = [], [], [], []
    for p in range(npb):
        t_out = (t_acc[p] / soft[p, 2:3, :]).astype(jnp.bfloat16).astype(jnp.float32)
        s_out = (s_acc[p] / soft[p, 3:4, :]).astype(jnp.bfloat16).astype(jnp.float32)
        t_acc[p] = t_out
        s_acc[p] = s_out
        t_sums.append(by_token(jnp.sum(t_out * t_out, axis=0, keepdims=True)))
        s_sums.append(by_token(jnp.sum(s_out * s_out, axis=0, keepdims=True)))

    plane = npb * nha
    slot = pb * nha + ha

    def share(buffer, send, recv, r):
        to = (slot + r) % plane
        return pltpu.make_async_remote_copy(
            src_ref=buffer.at[slot],
            dst_ref=buffer.at[slot],
            send_sem=send.at[r],
            recv_sem=recv.at[r],
            device_id=(to // nha, z, to % nha),
            device_id_type=MESH,
        )

    stats[slot] = jnp.concatenate(t_sums + s_sums, axis=0)
    for r in range(1, plane):
        share(stats, stat_send, stat_recv, r).start()
    for r in range(1, plane):
        share(stats, stat_send, stat_recv, r).wait_recv()
    sums = stats[0]
    for i in range(1, plane):
        sums = sums + stats[i]
    t_scale = lax.rsqrt(sums[0:npb] * (1.0 / (heads * plane * TD)) + EPSILON)
    s_scale = lax.rsqrt(sums[npb : 2 * npb] * (1.0 / (heads * plane * SD)) + EPSILON)

    loss = jnp.zeros((1, npb * rows), jnp.float32)
    first_head = (ha * npb + pb) * heads
    features, differences = [], []
    for j in range(heads):
        cut = slice(j * rows, (j + 1) * rows)
        target = jnp.concatenate(
            [t_acc[p, :, cut] * t_scale[p : p + 1] for p in range(npb)], axis=1
        )
        feature = jnp.concatenate(
            [s_acc[p, :, cut] * s_scale[p : p + 1] for p in range(npb)], axis=1
        ).astype(jnp.bfloat16)
        difference = columns_dot(w_ref[first_head + j], feature) - target
        loss = loss + jnp.sum(difference * difference, axis=0, keepdims=True)
        features.append(feature)
        differences.append(difference)
    losses[slot] = jnp.concatenate(
        [loss[:, p * rows : (p + 1) * rows] for p in range(npb)]
        + [jnp.zeros((8 - npb, rows), jnp.float32)],
        axis=0,
    )
    for r in range(1, plane):
        share(losses, loss_send, loss_recv, r).start()

    def grad_copy(j):
        return pltpu.make_async_remote_copy(
            src_ref=grads.at[j],
            dst_ref=grads_in.at[z],
            send_sem=grad_send.at[j],
            recv_sem=grad_recv.at[z],
            device_id=coords(first_head + j),
            device_id_type=MESH,
        )

    for j in range(heads):
        high = differences[j].astype(jnp.bfloat16)
        low = (differences[j] - high.astype(jnp.float32)).astype(jnp.bfloat16)
        grads[j] = rows_dot(features[j], high) + rows_dot(features[j], low)

        @pl.when(first_head + j != me)
        def _():
            grad_copy(j).start()

        @pl.when(first_head + j == me)
        def _():
            grads_in[z] = grads[j]

    for r in range(1, plane):
        share(losses, loss_send, loss_recv, r).wait_recv()
    mine = losses[0, pl.ds(pb, 1), :]
    for i in range(1, plane):
        mine = mine + losses[i, pl.ds(pb, 1), :]
    part = rows // nha
    chosen = mine[:, 0:part]
    for i in range(1, nha):
        chosen = jnp.where(ha == i, mine[:, i * part : (i + 1) * part], chosen)
    loss_ref[...] = chosen * (1.0 / (heads * plane * TD))

    giver_ha = me // (npb * heads)
    giver_pb = (me // heads) % npb
    for i in range(nkv):

        @pl.when((giver_ha != ha) | (giver_pb != pb) | (z != i))
        def _():
            pltpu.make_async_remote_copy(
                src_ref=grads.at[0],
                dst_ref=grads_in.at[i],
                send_sem=grad_send.at[0],
                recv_sem=grad_recv.at[i],
                device_id=(giver_pb, i, giver_ha),
                device_id_type=MESH,
            ).wait_recv()

    total = grads_in[0]
    for i in range(1, nkv):
        total = total + grads_in[i]
    grad_ref[...] = total * (1.0 / math.sqrt(tokens))

    for r in range(1, npb):
        kv_copy(r).wait_send()
        q_copy(r, 0).wait_send()
        q_copy(r, 1).wait_send()
    for h in range(nkv - 1):
        for r in range(npb):

            @pl.when((z - h >= 0) & (z < nkv - 1))
            def _():
                chain(h, r, True).wait_send()

            @pl.when((z + h <= nkv - 1) & (z > 0))
            def _():
                chain(h, r, False).wait_send()

    for r in range(1, plane):
        share(stats, stat_send, stat_recv, r).wait_send()
        share(losses, loss_send, loss_recv, r).wait_send()
    for j in range(heads):

        @pl.when(first_head + j != me)
        def _():
            grad_copy(j).wait_send()


def by_heads(
    shape, teacher_q, teacher_k, teacher_v, student_q, student_k, student_v, doc_ids, proj_weight
):
    npb, nkv, nha = shape
    rows = teacher_q.shape[0]
    heads = teacher_q.shape[1] // (npb * TD)
    wide = heads * rows
    plane = npb * nha
    dma = pltpu.SemaphoreType.DMA
    bf16, f32 = jnp.bfloat16, jnp.float32
    vmem = pl.BlockSpec(memory_space=pltpu.VMEM)
    grad, loss = pl.pallas_call(
        functools.partial(fused, shape, rows * npb * nkv),
        out_shape=(
            jax.ShapeDtypeStruct((SD, TD), f32),
            jax.ShapeDtypeStruct((1, rows // nha), f32),
        ),
        in_specs=[vmem] * 8,
        out_specs=(vmem, vmem),
        scratch_shapes=[
            pltpu.VMEM((npb, 3 * rows + 16, TD), bf16),
            pltpu.VMEM((nkv, npb, 3 * rows + 16, TD), bf16),
            pltpu.VMEM((npb, rows, heads * TD), bf16),
            pltpu.VMEM((npb, rows, heads * SD), bf16),
            pltpu.VMEM((npb, wide, TD), bf16),
            pltpu.VMEM((npb, wide, TD), bf16),
            pltpu.VMEM((npb, TD, wide), f32),
            pltpu.VMEM((npb, SD, wide), f32),
            pltpu.VMEM((npb, 8, wide), f32),
            pltpu.VMEM((plane, 8, rows), f32),
            pltpu.VMEM((plane, 8, rows), f32),
            pltpu.VMEM((heads, SD, TD), f32),
            pltpu.VMEM((nkv, SD, TD), f32),
            dma((npb,)),
            dma((npb,)),
            dma((npb, 2)),
            dma((npb, 2)),
            dma((nkv, npb)),
            dma((nkv, npb)),
            dma((nkv, npb)),
            dma((nkv, npb)),
            dma((plane,)),
            dma((plane,)),
            dma((plane,)),
            dma((plane,)),
            dma((heads,)),
            dma((nkv,)),
        ],
        compiler_params=pltpu.CompilerParams(
            collective_id=0, has_side_effects=True, vmem_limit_bytes=48 * 1024 * 1024
        ),
        name="attention_distillation",
    )(
        teacher_q,
        teacher_k,
        teacher_v,
        student_q,
        student_k,
        student_v,
        doc_ids.reshape(1, rows),
        proj_weight,
    )
    return grad, loss.reshape(-1)


def local(*arguments):
    teacher_q, teacher_k, proj_weight = arguments[0], arguments[1], arguments[7]
    shape = tuple(lax.axis_size(name) for name in ("pb", "kv", "ha"))
    groups = teacher_k.shape[1] // TD
    fits = (
        groups == shape[0] == 4
        and shape[2] == 2
        and math.prod(shape) == proj_weight.shape[0]
        and teacher_q.shape[0] == 128
    )
    if fits:
        return by_heads(shape, *arguments)
    return gathered(*arguments)


def solution(mesh):
    in_specs = (
        P(("pb", "kv"), "ha"),
        P(("pb", "kv"), "ha"),
        P(("pb", "kv"), "ha"),
        P(("pb", "kv"), "ha"),
        P(("pb", "kv"), "ha"),
        P(("pb", "kv"), "ha"),
        P(("pb", "kv")),
        P(),
    )
    out_specs = (P(("pb", "kv", "ha"), None), P(("pb", "kv", "ha")))
    return jax.shard_map(local, mesh=mesh, in_specs=in_specs, out_specs=out_specs, check_vma=False)
```

```python
import functools
import math

import jax
import jax.numpy as jnp
from jax import lax
from jax.experimental import pallas as pl
from jax.experimental.pallas import tpu as pltpu
from jax.sharding import PartitionSpec as P

MESH = pl.DeviceIdType.MESH

TD = 128
SD = 64
DOCS = 4


NEGATIVE = -1e30
EPSILON = 1e-06


def start_state(queries, head_size, groups):
    queried = queries.shape[0]
    per_group = queries.shape[1] // (groups * head_size)
    largest = jnp.full((groups, per_group, queried), NEGATIVE, jnp.float32)
    totals = jnp.zeros((groups, per_group, queried), jnp.float32)
    accum = jnp.zeros((groups, per_group, queried, head_size), jnp.float32)
    return (largest, totals, accum)


def attend_keys(
    state, queries, query_pos, query_doc, keys_piece, values_piece, key_pos, key_doc, head_size
):
    length = keys_piece.shape[0]
    block = math.gcd(length, 512)
    blocks = length // block
    groups = keys_piece.shape[1] // head_size
    queried = queries.shape[0]
    per_group = queries.shape[1] // (groups * head_size)
    shaped = queries.reshape(queried, groups, per_group, head_size)
    scale = 1.0 / math.sqrt(head_size)
    newest = jnp.max(query_pos)

    def compute(current, key_block, value_block, pos_block, doc_block):
        largest, totals, accum = current
        scores = (
            jnp.einsum(
                "qgpd,kgd->gpqk",
                shaped,
                key_block.reshape(block, groups, head_size),
                preferred_element_type=jnp.float32,
            )
            * scale
        )
        allowed = (query_doc[:, None] == doc_block[None, :]) & (
            pos_block[None, :] <= query_pos[:, None]
        )
        scores = jnp.where(allowed, scores, NEGATIVE)
        updated = jnp.maximum(largest, jnp.max(scores, axis=-1))
        weights = jnp.where(allowed, jnp.exp(scores - updated[..., None]), 0.0)
        factor = jnp.exp(largest - updated)
        totals = totals * factor + jnp.sum(weights, axis=-1)
        mixed = jnp.einsum(
            "gpqk,kgd->gpqd",
            weights.astype(jnp.bfloat16),
            value_block.reshape(block, groups, head_size),
            preferred_element_type=jnp.float32,
        )
        return (updated, totals, accum * factor[..., None] + mixed)

    def visit(current, item):
        key_block, value_block, pos_block, doc_block = item
        result = lax.cond(
            pos_block[0] <= newest,
            lambda inner: compute(inner, key_block, value_block, pos_block, doc_block),
            lambda inner: inner,
            current,
        )
        return (result, None)

    items = (
        keys_piece.reshape(blocks, block, -1),
        values_piece.reshape(blocks, block, -1),
        key_pos.reshape(blocks, block),
        key_doc.reshape(blocks, block),
    )
    final, unused = lax.scan(visit, state, items)
    return final


def finish(totals, accum):
    queried = accum.shape[2]
    result = accum / totals[..., None]
    return jnp.transpose(result, (2, 0, 1, 3)).reshape(queried, -1).astype(jnp.bfloat16)


def gathered(teacher_q, teacher_k, teacher_v, student_q, student_k, student_v, doc_ids, proj_weight):
    shard_rows = teacher_q.shape[0]
    groups = teacher_k.shape[1] // TD
    outer = lax.axis_size("pb")
    inner_size = lax.axis_size("kv")
    total_tokens = shard_rows * outer * inner_size
    shard = lax.axis_index("pb") * inner_size + lax.axis_index("kv")
    own_pos = shard * shard_rows + jnp.arange(shard_rows, dtype=jnp.int32)
    initial = (start_state(teacher_q, TD, groups), start_state(student_q, SD, groups))
    key_teacher = lax.all_gather(teacher_k, ("pb", "kv"), axis=0, tiled=True)
    value_teacher = lax.all_gather(teacher_v, ("pb", "kv"), axis=0, tiled=True)
    key_student = lax.all_gather(student_k, ("pb", "kv"), axis=0, tiled=True)
    value_student = lax.all_gather(student_v, ("pb", "kv"), axis=0, tiled=True)
    piece_doc = lax.all_gather(doc_ids, ("pb", "kv"), axis=0, tiled=True)
    key_pos = jnp.arange(piece_doc.shape[0], dtype=jnp.int32)
    teacher_state = attend_keys(
        initial[0], teacher_q, own_pos, doc_ids, key_teacher, value_teacher, key_pos, piece_doc, TD
    )
    student_state = attend_keys(
        initial[1], student_q, own_pos, doc_ids, key_student, value_student, key_pos, piece_doc, SD
    )
    teacher_state, student_state = (teacher_state, student_state)
    teacher_out = finish(teacher_state[1], teacher_state[2])
    student_out = finish(student_state[1], student_state[2])
    teacher_half, student_half = (
        lax.all_to_all(teacher_out, "ha", split_axis=0, concat_axis=1, tiled=True),
        lax.all_to_all(student_out, "ha", split_axis=0, concat_axis=1, tiled=True),
    )
    count = teacher_half.shape[0]
    heads = proj_weight.shape[0]
    teacher_float = teacher_half.astype(jnp.float32)
    target = teacher_float * lax.rsqrt(
        jnp.mean(teacher_float * teacher_float, axis=1, keepdims=True) + EPSILON
    )
    student_float = student_half.astype(jnp.float32)
    features = (
        student_float
        * lax.rsqrt(jnp.mean(student_float * student_float, axis=1, keepdims=True) + EPSILON)
    ).astype(jnp.bfloat16)
    feature_heads = features.reshape(count, heads, -1)
    predicted = jnp.einsum(
        "thd,hde->the", feature_heads, proj_weight, preferred_element_type=jnp.float32
    )
    difference = predicted.reshape(count, -1) - target
    token_loss = jnp.mean(difference * difference, axis=1)
    gradient = jnp.einsum(
        "thd,the->hde",
        feature_heads.astype(jnp.float32),
        difference.reshape(count, heads, -1),
        precision=lax.Precision.HIGHEST,
    )
    gradient = (gradient / math.sqrt(total_tokens)).reshape(-1, gradient.shape[2])
    grad_w = lax.psum_scatter(gradient, ("pb", "kv", "ha"), scatter_dimension=0, tiled=True)
    return (grad_w, token_loss)

def rows_dot(a, b):
    return lax.dot_general(a, b, (((1,), (1,)), ((), ())), preferred_element_type=jnp.float32)


def columns_dot(a, b):
    return lax.dot_general(a, b, (((0,), (0,)), ((), ())), preferred_element_type=jnp.float32)


def fused(
    shape,
    tokens,
    tq_ref,
    tk_hbm,
    tv_hbm,
    sq_ref,
    sk_hbm,
    sv_hbm,
    doc_hbm,
    w_hbm,
    grad_ref,
    loss_ref,
    tk_ref,
    tv_ref,
    sk_ref,
    sv_ref,
    doc_ref,
    w_ref,
    stage,
    kv,
    tq_in,
    sq_in,
    tq_all,
    sq_all,
    t_acc,
    s_acc,
    soft,
    stats,
    losses,
    grads,
    grads_in,
    xy_send,
    xy_recv,
    q_send,
    q_recv,
    up_send,
    up_recv,
    down_send,
    down_recv,
    stat_send,
    stat_recv,
    loss_send,
    loss_recv,
    grad_send,
    grad_recv,
    load_sem,
):
    npb, nkv, nha = shape
    devices = npb * nkv * nha
    rows = tq_ref.shape[0]
    heads = tq_ref.shape[1] // (npb * TD)
    wide = heads * rows
    pb, z, ha = lax.axis_index("pb"), lax.axis_index("kv"), lax.axis_index("ha")
    me = (pb * nkv + z) * nha + ha

    def coords(index):
        return (index // (nkv * nha), (index // nha) % nkv, index % nha)

    first_head = (ha * npb + pb) * heads

    def query_part(place, which):
        ref, width = ((tq_ref, heads * TD), (sq_ref, heads * SD))[which]
        return ref.at[:, pl.ds(pl.multiple_of(place * width, width), width)]

    loads = [
        pltpu.make_async_copy(source, into, load_sem.at[i])
        for i, (source, into) in enumerate(
            (
                (tk_hbm, tk_ref),
                (tv_hbm, tv_ref),
                (sk_hbm, sk_ref),
                (sv_hbm, sv_ref),
                (doc_hbm, doc_ref),
                (w_hbm.at[pl.ds(first_head, heads)], w_ref),
                (query_part(pb, 0), tq_in.at[pb]),
                (query_part(pb, 1), sq_in.at[pb]),
            )
        )
    ]
    for load in loads:
        load.start()

    barrier = pltpu.get_barrier_semaphore()

    def greet(r, carry):
        pl.semaphore_signal(
            barrier, inc=1, device_id=coords((me + r) % devices), device_id_type=MESH
        )
        return carry

    lax.fori_loop(1, devices, greet, 0)

    for load in loads[:5]:
        load.wait()
    doc_rows = jnp.broadcast_to(doc_ref[...].astype(jnp.float32), (16, rows)).astype(jnp.bfloat16)
    for g in range(npb):
        stage[g, 0:rows, :] = tk_ref[:, g * TD : (g + 1) * TD]
        stage[g, rows : 2 * rows, :] = tv_ref[:, g * TD : (g + 1) * TD]
        stage[g, 2 * rows : 3 * rows, :] = jnp.concatenate(
            [sk_ref[:, g * SD : (g + 1) * SD], sv_ref[:, g * SD : (g + 1) * SD]], axis=1
        )
        stage[g, 3 * rows : 3 * rows + 16, :] = doc_rows
    kv[z, pb] = stage[pb]

    pl.semaphore_wait(barrier, devices - 1)

    def partner(r):
        return ((pb // 2 + r // 2) % 2) * 2 + (pb % 2 + r % 2) % 2

    def kv_copy(r):
        to = partner(r)
        return pltpu.make_async_remote_copy(
            src_ref=stage.at[to],
            dst_ref=kv.at[z, pb],
            send_sem=xy_send.at[r],
            recv_sem=xy_recv.at[r],
            device_id=(to, z, ha),
            device_id_type=MESH,
        )

    def q_copy(r, which):
        to = partner(r)
        return pltpu.make_async_remote_copy(
            src_ref=query_part(to, which),
            dst_ref=(tq_in, sq_in)[which].at[pb],
            send_sem=q_send.at[r, which],
            recv_sem=q_recv.at[r, which],
            device_id=(to, z, ha),
            device_id_type=MESH,
        )

    for r in range(1, npb):
        kv_copy(r).start()

    def chain(h, c, up):
        piece = kv.at[z - h if up else z + h, c]
        send, recv = (up_send, up_recv) if up else (down_send, down_recv)
        return pltpu.make_async_remote_copy(
            src_ref=piece,
            dst_ref=piece,
            send_sem=send.at[h, c],
            recv_sem=recv.at[h, c],
            device_id=(pb, z + 1 if up else z - 1, ha),
            device_id_type=MESH,
        )

    def arrived(h, c, up):
        piece = kv.at[z - h if up else z + h, c]
        send, recv = (up_send, up_recv) if up else (down_send, down_recv)
        pltpu.make_async_remote_copy(
            src_ref=piece,
            dst_ref=piece,
            send_sem=send.at[h - 1, c],
            recv_sem=recv.at[h - 1, c],
            device_id=(pb, z - 1 if up else z + 1, ha),
            device_id_type=MESH,
        ).wait_recv()

    for r in range(npb):
        if r > 0:
            kv_copy(r).wait_recv()

        @pl.when(z < nkv - 1)
        def _():
            chain(0, partner(r), True).start()

        @pl.when((z > 0) & (partner(r) < npb - 1))
        def _():
            chain(0, partner(r), False).start()

    for r in range(1, npb):
        q_copy(r, 0).start()
        q_copy(r, 1).start()

    def next_hop(h, c):
        @pl.when(z - h >= 0)
        def _():
            arrived(h, c, True)

            @pl.when(z < nkv - 1)
            def _():
                chain(h, c, True).start()

        if c < npb - 1:

            @pl.when(z + h <= nkv - 1)
            def _():
                arrived(h, c, False)

                @pl.when(z > 0)
                def _():
                    chain(h, c, False).start()

    for c in range(npb):
        next_hop(1, c)

    for load in loads[5:]:
        load.wait()
    for r in range(1, npb):
        q_copy(r, 0).wait_recv()
        q_copy(r, 1).wait_recv()
    blank = jnp.zeros((rows, TD - SD), jnp.bfloat16)
    for p in range(npb):
        for j in range(heads):
            tq_all[p, j * rows : (j + 1) * rows, :] = tq_in[p, :, j * TD : (j + 1) * TD]
            sq_all[p, j * rows : (j + 1) * rows, :] = jnp.concatenate(
                [sq_in[p, :, j * SD : (j + 1) * SD], blank], axis=1
            )
    t_acc[...] = jnp.zeros_like(t_acc)
    s_acc[...] = jnp.zeros_like(s_acc)
    soft[:, 0:2, :] = jnp.full((npb, 2, wide), NEGATIVE, jnp.float32)
    soft[:, 2:4, :] = jnp.zeros((npb, 2, wide), jnp.float32)

    local_key = lax.broadcasted_iota(jnp.int32, (rows, wide), 0)
    local_query = lax.broadcasted_iota(jnp.int32, (1, wide), 1) % rows

    def attend(source, p, count):
        keys = count * rows
        own = kv[z, p, 3 * rows : 3 * rows + 16, :].astype(jnp.float32)[0:1, :]
        query_doc = jnp.concatenate([own] * heads, axis=1)
        allowed = []
        for c in range(count):
            key_doc = kv[source, c, 3 * rows : 3 * rows + 16, :].astype(jnp.float32)[0:1, :]
            least = jnp.zeros((1, wide), jnp.float32)
            for d in range(1, DOCS):
                before = jnp.sum((key_doc < d).astype(jnp.float32), axis=1, keepdims=True)
                least = jnp.where(query_doc == d, before, least)
            ok = local_key >= least.astype(jnp.int32)
            if c == p:
                ok = ok & (local_key <= local_query + (z - source) * rows)
            allowed.append(ok)
        for which in range(2):
            factor = math.log2(math.e) / math.sqrt((TD, SD)[which])
            queries = (tq_all, sq_all)[which][p]
            if which == 0:
                key_rows = kv[source, 0:count, 0:rows, :].reshape(keys, TD)
                value_rows = kv[source, 0:count, rows : 2 * rows, :].reshape(keys, TD)
            else:
                key_rows = kv[source, 0:count, 2 * rows : 3 * rows, :].reshape(keys, TD)
                value_rows = key_rows
            raw = rows_dot(key_rows, queries)
            scores = jnp.concatenate(
                [
                    jnp.where(allowed[c], raw[c * rows : (c + 1) * rows], NEGATIVE)
                    for c in range(count)
                ],
                axis=0,
            )
            old = soft[p, which : which + 1, :]
            new = jnp.maximum(old, jnp.max(scores, axis=0, keepdims=True))
            weights = jnp.exp2((scores - new) * factor)
            shrink = jnp.exp2((old - new) * factor)
            soft[p, which : which + 1, :] = new
            soft[p, which + 2 : which + 3, :] = soft[
                p, which + 2 : which + 3, :
            ] * shrink + jnp.sum(weights, axis=0, keepdims=True)
            mixed = columns_dot(value_rows, weights.astype(jnp.bfloat16))
            if which == 0:
                t_acc[p] = t_acc[p] * shrink + mixed
            else:
                s_acc[p] = s_acc[p] * shrink + mixed[TD - SD :]

    def turn(h, carry):
        for p in range(npb):

            @pl.when(h >= 2)
            def _():
                next_hop(h, p)

            @pl.when(z - h >= 0)
            def _():
                attend(z - h, p, p + 1)

            if p > 0:

                @pl.when((z + h <= nkv - 1) & (h > 0))
                def _():
                    attend(z + h, p, p)

        return carry

    lax.fori_loop(0, nkv, turn, 0)

    def by_token(row):
        total = row[:, 0:rows]
        for j in range(1, heads):
            total = total + row[:, j * rows : (j + 1) * rows]
        return total

    t_sums, s_sums, t_outs, s_outs = [], [], [], []
    for p in range(npb):
        t_out = (t_acc[p] / soft[p, 2:3, :]).astype(jnp.bfloat16).astype(jnp.float32)
        s_out = (s_acc[p] / soft[p, 3:4, :]).astype(jnp.bfloat16).astype(jnp.float32)
        t_acc[p] = t_out
        s_acc[p] = s_out
        t_sums.append(by_token(jnp.sum(t_out * t_out, axis=0, keepdims=True)))
        s_sums.append(by_token(jnp.sum(s_out * s_out, axis=0, keepdims=True)))

    plane = npb * nha
    slot = pb * nha + ha

    def share(buffer, send, recv, r):
        to = (slot + r) % plane
        return pltpu.make_async_remote_copy(
            src_ref=buffer.at[slot],
            dst_ref=buffer.at[slot],
            send_sem=send.at[r],
            recv_sem=recv.at[r],
            device_id=(to // nha, z, to % nha),
            device_id_type=MESH,
        )

    stats[slot] = jnp.concatenate(t_sums + s_sums, axis=0)
    for r in range(1, plane):
        share(stats, stat_send, stat_recv, r).start()
    for r in range(1, plane):
        share(stats, stat_send, stat_recv, r).wait_recv()
    sums = stats[0]
    for i in range(1, plane):
        sums = sums + stats[i]
    t_scale = lax.rsqrt(sums[0:npb] * (1.0 / (heads * plane * TD)) + EPSILON)
    s_scale = lax.rsqrt(sums[npb : 2 * npb] * (1.0 / (heads * plane * SD)) + EPSILON)

    loss = jnp.zeros((1, npb * rows), jnp.float32)
    features, differences = [], []
    for j in range(heads):
        cut = slice(j * rows, (j + 1) * rows)
        target = jnp.concatenate(
            [t_acc[p, :, cut] * t_scale[p : p + 1] for p in range(npb)], axis=1
        )
        feature = jnp.concatenate(
            [s_acc[p, :, cut] * s_scale[p : p + 1] for p in range(npb)], axis=1
        ).astype(jnp.bfloat16)
        difference = columns_dot(w_ref[j], feature) - target
        loss = loss + jnp.sum(difference * difference, axis=0, keepdims=True)
        features.append(feature)
        differences.append(difference)
    losses[slot] = jnp.concatenate(
        [loss[:, p * rows : (p + 1) * rows] for p in range(npb)]
        + [jnp.zeros((8 - npb, rows), jnp.float32)],
        axis=0,
    )
    for r in range(1, plane):
        share(losses, loss_send, loss_recv, r).start()

    def grad_copy(j):
        return pltpu.make_async_remote_copy(
            src_ref=grads.at[j],
            dst_ref=grads_in.at[z],
            send_sem=grad_send.at[j],
            recv_sem=grad_recv.at[z],
            device_id=coords(first_head + j),
            device_id_type=MESH,
        )

    for j in range(heads):
        high = differences[j].astype(jnp.bfloat16)
        low = (differences[j] - high.astype(jnp.float32)).astype(jnp.bfloat16)
        grads[j] = rows_dot(features[j], high) + rows_dot(features[j], low)

        @pl.when(first_head + j != me)
        def _():
            grad_copy(j).start()

        @pl.when(first_head + j == me)
        def _():
            grads_in[z] = grads[j]

    for r in range(1, plane):
        share(losses, loss_send, loss_recv, r).wait_recv()
    mine = losses[0, pl.ds(pb, 1), :]
    for i in range(1, plane):
        mine = mine + losses[i, pl.ds(pb, 1), :]
    part = rows // nha
    chosen = mine[:, 0:part]
    for i in range(1, nha):
        chosen = jnp.where(ha == i, mine[:, i * part : (i + 1) * part], chosen)
    loss_ref[...] = chosen * (1.0 / (heads * plane * TD))

    giver_ha = me // (npb * heads)
    giver_pb = (me // heads) % npb
    for i in range(nkv):

        @pl.when((giver_ha != ha) | (giver_pb != pb) | (z != i))
        def _():
            pltpu.make_async_remote_copy(
                src_ref=grads.at[0],
                dst_ref=grads_in.at[i],
                send_sem=grad_send.at[0],
                recv_sem=grad_recv.at[i],
                device_id=(giver_pb, i, giver_ha),
                device_id_type=MESH,
            ).wait_recv()

    total = grads_in[0]
    for i in range(1, nkv):
        total = total + grads_in[i]
    grad_ref[...] = total * (1.0 / math.sqrt(tokens))

    for r in range(1, npb):
        kv_copy(r).wait_send()
        q_copy(r, 0).wait_send()
        q_copy(r, 1).wait_send()
    for h in range(nkv - 1):
        for c in range(npb):

            @pl.when((z - h >= 0) & (z < nkv - 1))
            def _():
                chain(h, c, True).wait_send()

            if c < npb - 1:

                @pl.when((z + h <= nkv - 1) & (z > 0))
                def _():
                    chain(h, c, False).wait_send()

    for r in range(1, plane):
        share(stats, stat_send, stat_recv, r).wait_send()
        share(losses, loss_send, loss_recv, r).wait_send()
    for j in range(heads):

        @pl.when(first_head + j != me)
        def _():
            grad_copy(j).wait_send()


def by_heads(
    shape, teacher_q, teacher_k, teacher_v, student_q, student_k, student_v, doc_ids, proj_weight
):
    npb, nkv, nha = shape
    rows = teacher_q.shape[0]
    heads = teacher_q.shape[1] // (npb * TD)
    wide = heads * rows
    plane = npb * nha
    dma = pltpu.SemaphoreType.DMA
    bf16, f32 = jnp.bfloat16, jnp.float32
    vmem = pl.BlockSpec(memory_space=pltpu.VMEM)
    grad, loss = pl.pallas_call(
        functools.partial(fused, shape, rows * npb * nkv),
        out_shape=(
            jax.ShapeDtypeStruct((SD, TD), f32),
            jax.ShapeDtypeStruct((1, rows // nha), f32),
        ),
        in_specs=[pl.BlockSpec(memory_space=pltpu.HBM)] * 8,
        out_specs=(vmem, vmem),
        scratch_shapes=[
            pltpu.VMEM(teacher_k.shape, bf16),
            pltpu.VMEM(teacher_v.shape, bf16),
            pltpu.VMEM(student_k.shape, bf16),
            pltpu.VMEM(student_v.shape, bf16),
            pltpu.VMEM((1, rows), jnp.int32),
            pltpu.VMEM((heads, SD, TD), bf16),
            pltpu.VMEM((npb, 3 * rows + 16, TD), bf16),
            pltpu.VMEM((nkv, npb, 3 * rows + 16, TD), bf16),
            pltpu.VMEM((npb, rows, heads * TD), bf16),
            pltpu.VMEM((npb, rows, heads * SD), bf16),
            pltpu.VMEM((npb, wide, TD), bf16),
            pltpu.VMEM((npb, wide, TD), bf16),
            pltpu.VMEM((npb, TD, wide), f32),
            pltpu.VMEM((npb, SD, wide), f32),
            pltpu.VMEM((npb, 8, wide), f32),
            pltpu.VMEM((plane, 8, rows), f32),
            pltpu.VMEM((plane, 8, rows), f32),
            pltpu.VMEM((heads, SD, TD), f32),
            pltpu.VMEM((nkv, SD, TD), f32),
            dma((npb,)),
            dma((npb,)),
            dma((npb, 2)),
            dma((npb, 2)),
            dma((nkv, npb)),
            dma((nkv, npb)),
            dma((nkv, npb)),
            dma((nkv, npb)),
            dma((plane,)),
            dma((plane,)),
            dma((plane,)),
            dma((plane,)),
            dma((heads,)),
            dma((nkv,)),
            dma((8,)),
        ],
        compiler_params=pltpu.CompilerParams(
            collective_id=0, has_side_effects=True, vmem_limit_bytes=63 * 1024 * 1024
        ),
        name="attention_distillation",
    )(
        teacher_q,
        teacher_k,
        teacher_v,
        student_q,
        student_k,
        student_v,
        doc_ids.reshape(1, rows),
        proj_weight,
    )
    return grad, loss.reshape(-1)


def local(*arguments):
    teacher_q, teacher_k, proj_weight = arguments[0], arguments[1], arguments[7]
    shape = tuple(lax.axis_size(name) for name in ("pb", "kv", "ha"))
    groups = teacher_k.shape[1] // TD
    fits = (
        groups == shape[0] == 4
        and shape[2] == 2
        and math.prod(shape) == proj_weight.shape[0]
        and teacher_q.shape[0] == 128
    )
    if fits:
        return by_heads(shape, *arguments)
    return gathered(*arguments)


def solution(mesh):
    in_specs = (
        P(("pb", "kv"), "ha"),
        P(("pb", "kv"), "ha"),
        P(("pb", "kv"), "ha"),
        P(("pb", "kv"), "ha"),
        P(("pb", "kv"), "ha"),
        P(("pb", "kv"), "ha"),
        P(("pb", "kv")),
        P(),
    )
    out_specs = (P(("pb", "kv", "ha"), None), P(("pb", "kv", "ha")))
    return jax.shard_map(local, mesh=mesh, in_specs=in_specs, out_specs=out_specs, check_vma=False)
```

```python
import functools
import math

import jax
import jax.numpy as jnp
from jax import lax
from jax.experimental import pallas as pl
from jax.experimental.pallas import tpu as pltpu
from jax.sharding import PartitionSpec as P

MESH = pl.DeviceIdType.MESH

TD = 128
SD = 64
DOCS = 4


NEGATIVE = -1e30
EPSILON = 1e-06


def start_state(queries, head_size, groups):
    queried = queries.shape[0]
    per_group = queries.shape[1] // (groups * head_size)
    largest = jnp.full((groups, per_group, queried), NEGATIVE, jnp.float32)
    totals = jnp.zeros((groups, per_group, queried), jnp.float32)
    accum = jnp.zeros((groups, per_group, queried, head_size), jnp.float32)
    return (largest, totals, accum)


def attend_keys(
    state, queries, query_pos, query_doc, keys_piece, values_piece, key_pos, key_doc, head_size
):
    length = keys_piece.shape[0]
    block = math.gcd(length, 512)
    blocks = length // block
    groups = keys_piece.shape[1] // head_size
    queried = queries.shape[0]
    per_group = queries.shape[1] // (groups * head_size)
    shaped = queries.reshape(queried, groups, per_group, head_size)
    scale = 1.0 / math.sqrt(head_size)
    newest = jnp.max(query_pos)

    def compute(current, key_block, value_block, pos_block, doc_block):
        largest, totals, accum = current
        scores = (
            jnp.einsum(
                "qgpd,kgd->gpqk",
                shaped,
                key_block.reshape(block, groups, head_size),
                preferred_element_type=jnp.float32,
            )
            * scale
        )
        allowed = (query_doc[:, None] == doc_block[None, :]) & (
            pos_block[None, :] <= query_pos[:, None]
        )
        scores = jnp.where(allowed, scores, NEGATIVE)
        updated = jnp.maximum(largest, jnp.max(scores, axis=-1))
        weights = jnp.where(allowed, jnp.exp(scores - updated[..., None]), 0.0)
        factor = jnp.exp(largest - updated)
        totals = totals * factor + jnp.sum(weights, axis=-1)
        mixed = jnp.einsum(
            "gpqk,kgd->gpqd",
            weights.astype(jnp.bfloat16),
            value_block.reshape(block, groups, head_size),
            preferred_element_type=jnp.float32,
        )
        return (updated, totals, accum * factor[..., None] + mixed)

    def visit(current, item):
        key_block, value_block, pos_block, doc_block = item
        result = lax.cond(
            pos_block[0] <= newest,
            lambda inner: compute(inner, key_block, value_block, pos_block, doc_block),
            lambda inner: inner,
            current,
        )
        return (result, None)

    items = (
        keys_piece.reshape(blocks, block, -1),
        values_piece.reshape(blocks, block, -1),
        key_pos.reshape(blocks, block),
        key_doc.reshape(blocks, block),
    )
    final, unused = lax.scan(visit, state, items)
    return final


def finish(totals, accum):
    queried = accum.shape[2]
    result = accum / totals[..., None]
    return jnp.transpose(result, (2, 0, 1, 3)).reshape(queried, -1).astype(jnp.bfloat16)


def gathered(teacher_q, teacher_k, teacher_v, student_q, student_k, student_v, doc_ids, proj_weight):
    shard_rows = teacher_q.shape[0]
    groups = teacher_k.shape[1] // TD
    outer = lax.axis_size("pb")
    inner_size = lax.axis_size("kv")
    total_tokens = shard_rows * outer * inner_size
    shard = lax.axis_index("pb") * inner_size + lax.axis_index("kv")
    own_pos = shard * shard_rows + jnp.arange(shard_rows, dtype=jnp.int32)
    initial = (start_state(teacher_q, TD, groups), start_state(student_q, SD, groups))
    key_teacher = lax.all_gather(teacher_k, ("pb", "kv"), axis=0, tiled=True)
    value_teacher = lax.all_gather(teacher_v, ("pb", "kv"), axis=0, tiled=True)
    key_student = lax.all_gather(student_k, ("pb", "kv"), axis=0, tiled=True)
    value_student = lax.all_gather(student_v, ("pb", "kv"), axis=0, tiled=True)
    piece_doc = lax.all_gather(doc_ids, ("pb", "kv"), axis=0, tiled=True)
    key_pos = jnp.arange(piece_doc.shape[0], dtype=jnp.int32)
    teacher_state = attend_keys(
        initial[0], teacher_q, own_pos, doc_ids, key_teacher, value_teacher, key_pos, piece_doc, TD
    )
    student_state = attend_keys(
        initial[1], student_q, own_pos, doc_ids, key_student, value_student, key_pos, piece_doc, SD
    )
    teacher_state, student_state = (teacher_state, student_state)
    teacher_out = finish(teacher_state[1], teacher_state[2])
    student_out = finish(student_state[1], student_state[2])
    teacher_half, student_half = (
        lax.all_to_all(teacher_out, "ha", split_axis=0, concat_axis=1, tiled=True),
        lax.all_to_all(student_out, "ha", split_axis=0, concat_axis=1, tiled=True),
    )
    count = teacher_half.shape[0]
    heads = proj_weight.shape[0]
    teacher_float = teacher_half.astype(jnp.float32)
    target = teacher_float * lax.rsqrt(
        jnp.mean(teacher_float * teacher_float, axis=1, keepdims=True) + EPSILON
    )
    student_float = student_half.astype(jnp.float32)
    features = (
        student_float
        * lax.rsqrt(jnp.mean(student_float * student_float, axis=1, keepdims=True) + EPSILON)
    ).astype(jnp.bfloat16)
    feature_heads = features.reshape(count, heads, -1)
    predicted = jnp.einsum(
        "thd,hde->the", feature_heads, proj_weight, preferred_element_type=jnp.float32
    )
    difference = predicted.reshape(count, -1) - target
    token_loss = jnp.mean(difference * difference, axis=1)
    gradient = jnp.einsum(
        "thd,the->hde",
        feature_heads.astype(jnp.float32),
        difference.reshape(count, heads, -1),
        precision=lax.Precision.HIGHEST,
    )
    gradient = (gradient / math.sqrt(total_tokens)).reshape(-1, gradient.shape[2])
    grad_w = lax.psum_scatter(gradient, ("pb", "kv", "ha"), scatter_dimension=0, tiled=True)
    return (grad_w, token_loss)

def rows_dot(a, b):
    return lax.dot_general(a, b, (((1,), (1,)), ((), ())), preferred_element_type=jnp.float32)


def columns_dot(a, b):
    return lax.dot_general(a, b, (((0,), (0,)), ((), ())), preferred_element_type=jnp.float32)


def fused(
    shape,
    tokens,
    tq_ref,
    tk_hbm,
    tv_hbm,
    sq_ref,
    sk_hbm,
    sv_hbm,
    doc_hbm,
    w_hbm,
    grad_ref,
    loss_ref,
    tk_ref,
    tv_ref,
    sk_ref,
    sv_ref,
    doc_ref,
    w_ref,
    stage,
    kv,
    tq_in,
    sq_in,
    tq_all,
    sq_all,
    t_acc,
    s_acc,
    soft,
    stats,
    losses,
    grads,
    grads_in,
    xy_send,
    xy_recv,
    q_send,
    q_recv,
    up_send,
    up_recv,
    down_send,
    down_recv,
    stat_send,
    stat_recv,
    loss_send,
    loss_recv,
    grad_send,
    grad_recv,
    load_sem,
):
    npb, nkv, nha = shape
    devices = npb * nkv * nha
    rows = tq_ref.shape[0]
    heads = tq_ref.shape[1] // (npb * TD)
    wide = heads * rows
    pb, z, ha = lax.axis_index("pb"), lax.axis_index("kv"), lax.axis_index("ha")
    me = (pb * nkv + z) * nha + ha

    def coords(index):
        return (index // (nkv * nha), (index // nha) % nkv, index % nha)

    first_head = (ha * npb + pb) * heads

    def query_part(place, which):
        ref, width = ((tq_ref, heads * TD), (sq_ref, heads * SD))[which]
        return ref.at[:, pl.ds(pl.multiple_of(place * width, width), width)]

    loads = [
        pltpu.make_async_copy(source, into, load_sem.at[i])
        for i, (source, into) in enumerate(
            (
                (tk_hbm, tk_ref),
                (tv_hbm, tv_ref),
                (sk_hbm, sk_ref),
                (sv_hbm, sv_ref),
                (doc_hbm, doc_ref),
                (w_hbm.at[pl.ds(first_head, heads)], w_ref),
                (query_part(pb, 0), tq_in.at[pb]),
                (query_part(pb, 1), sq_in.at[pb]),
            )
        )
    ]
    for load in loads:
        load.start()

    barrier = pltpu.get_barrier_semaphore()

    def greet(r, carry):
        pl.semaphore_signal(
            barrier, inc=1, device_id=coords((me + r) % devices), device_id_type=MESH
        )
        return carry

    lax.fori_loop(1, devices, greet, 0)

    for load in loads[:5]:
        load.wait()
    doc_rows = jnp.broadcast_to(doc_ref[...].astype(jnp.float32), (16, rows)).astype(jnp.bfloat16)
    for g in range(npb):
        stage[g, 0:rows, :] = tk_ref[:, g * TD : (g + 1) * TD]
        stage[g, rows : 2 * rows, :] = (
            tv_ref[:, g * TD : (g + 1) * TD].astype(jnp.float32).T.astype(jnp.bfloat16)
        )
        stage[g, 2 * rows : 3 * rows, :] = jnp.concatenate(
            [sk_ref[:, g * SD : (g + 1) * SD], sv_ref[:, g * SD : (g + 1) * SD]], axis=1
        )
        stage[g, 3 * rows : 3 * rows + 16, :] = doc_rows
    kv[z, pb] = stage[pb]

    pl.semaphore_wait(barrier, devices - 1)

    def partner(r):
        return ((pb // 2 + r // 2) % 2) * 2 + (pb % 2 + r % 2) % 2

    def kv_copy(r):
        to = partner(r)
        return pltpu.make_async_remote_copy(
            src_ref=stage.at[to],
            dst_ref=kv.at[z, pb],
            send_sem=xy_send.at[r],
            recv_sem=xy_recv.at[r],
            device_id=(to, z, ha),
            device_id_type=MESH,
        )

    def q_copy(r, which):
        to = partner(r)
        return pltpu.make_async_remote_copy(
            src_ref=query_part(to, which),
            dst_ref=(tq_in, sq_in)[which].at[pb],
            send_sem=q_send.at[r, which],
            recv_sem=q_recv.at[r, which],
            device_id=(to, z, ha),
            device_id_type=MESH,
        )

    for r in range(1, npb):
        kv_copy(r).start()

    def chain(h, c, up):
        piece = kv.at[z - h if up else z + h, c]
        send, recv = (up_send, up_recv) if up else (down_send, down_recv)
        return pltpu.make_async_remote_copy(
            src_ref=piece,
            dst_ref=piece,
            send_sem=send.at[h, c],
            recv_sem=recv.at[h, c],
            device_id=(pb, z + 1 if up else z - 1, ha),
            device_id_type=MESH,
        )

    def arrived(h, c, up):
        piece = kv.at[z - h if up else z + h, c]
        send, recv = (up_send, up_recv) if up else (down_send, down_recv)
        pltpu.make_async_remote_copy(
            src_ref=piece,
            dst_ref=piece,
            send_sem=send.at[h - 1, c],
            recv_sem=recv.at[h - 1, c],
            device_id=(pb, z - 1 if up else z + 1, ha),
            device_id_type=MESH,
        ).wait_recv()

    for r in range(npb):
        if r > 0:
            kv_copy(r).wait_recv()

        @pl.when(z < nkv - 1)
        def _():
            chain(0, partner(r), True).start()

        @pl.when((z > 0) & (partner(r) < npb - 1))
        def _():
            chain(0, partner(r), False).start()

    for r in range(1, npb):
        q_copy(r, 0).start()
        q_copy(r, 1).start()

    def next_hop(h, c):
        @pl.when(z - h >= 0)
        def _():
            arrived(h, c, True)

            @pl.when(z < nkv - 1)
            def _():
                chain(h, c, True).start()

        if not isinstance(c, int) or c < npb - 1:

            @pl.when((z + h <= nkv - 1) & (c < npb - 1))
            def _():
                arrived(h, c, False)

                @pl.when(z > 0)
                def _():
                    chain(h, c, False).start()

    t_acc[...] = jnp.zeros_like(t_acc)
    s_acc[...] = jnp.zeros_like(s_acc)
    soft[:, 0:2, :] = jnp.full((npb, 2, wide), NEGATIVE, jnp.float32)
    soft[:, 2:4, :] = jnp.zeros((npb, 2, wide), jnp.float32)

    local_key = lax.broadcasted_iota(jnp.int32, (rows, wide), 0)
    local_query = lax.broadcasted_iota(jnp.int32, (1, wide), 1) % rows
    float_key = local_key.astype(jnp.float32)
    float_query = local_query.astype(jnp.float32)

    def attend(source, p, count, own_place=False):
        keys = count * rows
        own = kv[z, p, 3 * rows : 3 * rows + 16, :].astype(jnp.float32)[0:1, :]
        query_doc = jnp.concatenate([own] * heads, axis=1)
        firsts = []
        for c in range(count):
            key_doc = kv[source, c, 3 * rows : 3 * rows + 16, :].astype(jnp.float32)[0:1, :]
            least = jnp.zeros((1, wide), jnp.float32)
            for d in range(1, DOCS):
                before = jnp.sum((key_doc < d).astype(jnp.float32), axis=1, keepdims=True)
                least = jnp.where(query_doc == d, before, least)
            firsts.append(least)

        def allowed(c, which):
            if which == 0:
                ok = local_key >= firsts[c].astype(jnp.int32)
                return ok & (local_key <= local_query) if own_place and c == p else ok
            ok = float_key > firsts[c] - 0.5
            return ok & (float_key < float_query + 0.5) if own_place and c == p else ok

        for which in range(2):
            factor = math.log2(math.e) / math.sqrt((TD, SD)[which])
            queries = (tq_all, sq_all)[which][p]
            if which == 0:
                key_rows = kv[source, 0:count, 0:rows, :].reshape(keys, TD)
            else:
                key_rows = kv[source, 0:count, 2 * rows : 3 * rows, :].reshape(keys, TD)
            raw = rows_dot(key_rows, queries)
            scores = jnp.concatenate(
                [
                    jnp.where(allowed(c, which), raw[c * rows : (c + 1) * rows], NEGATIVE)
                    for c in range(count)
                ],
                axis=0,
            )
            old = soft[p, which : which + 1, :]
            new = jnp.maximum(old, jnp.max(scores, axis=0, keepdims=True))
            weights = jnp.exp2((scores - new) * factor)
            shrink = jnp.exp2((old - new) * factor)
            soft[p, which : which + 1, :] = new
            soft[p, which + 2 : which + 3, :] = soft[
                p, which + 2 : which + 3, :
            ] * shrink + jnp.sum(weights, axis=0, keepdims=True)
            rounded = weights.astype(jnp.bfloat16)
            if which == 0:
                values = jnp.concatenate(
                    [kv[source, c, rows : 2 * rows, :] for c in range(count)], axis=1
                )
                t_acc[p] = t_acc[p] * shrink + jnp.dot(
                    values, rounded, preferred_element_type=jnp.float32
                )
            else:
                s_acc[p] = s_acc[p] * shrink + columns_dot(key_rows, rounded)[TD - SD :]

    for load in loads[5:]:
        load.wait()
    blank = jnp.zeros((rows, TD - SD), jnp.bfloat16)

    def own_turn(r, carry):
        place = partner(r)
        next_hop(1, place)

        @pl.when(r > 0)
        def _():
            q_copy(r, 0).wait_recv()
            q_copy(r, 1).wait_recv()

        for j in range(heads):
            tq_all[place, j * rows : (j + 1) * rows, :] = tq_in[place, :, j * TD : (j + 1) * TD]
            sq_all[place, j * rows : (j + 1) * rows, :] = jnp.concatenate(
                [sq_in[place, :, j * SD : (j + 1) * SD], blank], axis=1
            )
        for p in range(npb):

            @pl.when(place == p)
            def _():
                attend(z, p, p + 1, True)

        return carry

    lax.fori_loop(0, npb, own_turn, 0)

    def turn(h, carry):
        for p in range(npb):

            @pl.when(h >= 2)
            def _():
                next_hop(h, p)

            @pl.when(z - h >= 0)
            def _():
                attend(z - h, p, p + 1)

            if p > 0:

                @pl.when(z + h <= nkv - 1)
                def _():
                    attend(z + h, p, p)

        return carry

    lax.fori_loop(1, nkv, turn, 0)

    def by_token(row):
        total = row[:, 0:rows]
        for j in range(1, heads):
            total = total + row[:, j * rows : (j + 1) * rows]
        return total

    t_sums, s_sums, t_outs, s_outs = [], [], [], []
    for p in range(npb):
        t_out = (t_acc[p] / soft[p, 2:3, :]).astype(jnp.bfloat16).astype(jnp.float32)
        s_out = (s_acc[p] / soft[p, 3:4, :]).astype(jnp.bfloat16).astype(jnp.float32)
        t_acc[p] = t_out
        s_acc[p] = s_out
        t_sums.append(by_token(jnp.sum(t_out * t_out, axis=0, keepdims=True)))
        s_sums.append(by_token(jnp.sum(s_out * s_out, axis=0, keepdims=True)))

    plane = npb * nha
    slot = pb * nha + ha

    def share(buffer, send, recv, r):
        to = (slot + r) % plane
        return pltpu.make_async_remote_copy(
            src_ref=buffer.at[slot],
            dst_ref=buffer.at[slot],
            send_sem=send.at[r],
            recv_sem=recv.at[r],
            device_id=(to // nha, z, to % nha),
            device_id_type=MESH,
        )

    stats[slot] = jnp.concatenate(t_sums + s_sums, axis=0)
    for r in range(1, plane):
        share(stats, stat_send, stat_recv, r).start()
    for r in range(1, plane):
        share(stats, stat_send, stat_recv, r).wait_recv()
    sums = stats[0]
    for i in range(1, plane):
        sums = sums + stats[i]
    t_scale = lax.rsqrt(sums[0:npb] * (1.0 / (heads * plane * TD)) + EPSILON)
    s_scale = lax.rsqrt(sums[npb : 2 * npb] * (1.0 / (heads * plane * SD)) + EPSILON)

    loss = jnp.zeros((1, npb * rows), jnp.float32)
    features, differences = [], []
    for j in range(heads):
        cut = slice(j * rows, (j + 1) * rows)
        target = jnp.concatenate(
            [t_acc[p, :, cut] * t_scale[p : p + 1] for p in range(npb)], axis=1
        )
        feature = jnp.concatenate(
            [s_acc[p, :, cut] * s_scale[p : p + 1] for p in range(npb)], axis=1
        ).astype(jnp.bfloat16)
        difference = columns_dot(w_ref[j], feature) - target
        loss = loss + jnp.sum(difference * difference, axis=0, keepdims=True)
        features.append(feature)
        differences.append(difference)
    losses[slot] = jnp.concatenate(
        [loss[:, p * rows : (p + 1) * rows] for p in range(npb)]
        + [jnp.zeros((8 - npb, rows), jnp.float32)],
        axis=0,
    )
    for r in range(1, plane):
        share(losses, loss_send, loss_recv, r).start()

    def grad_copy(j):
        return pltpu.make_async_remote_copy(
            src_ref=grads.at[j],
            dst_ref=grads_in.at[z],
            send_sem=grad_send.at[j],
            recv_sem=grad_recv.at[z],
            device_id=coords(first_head + j),
            device_id_type=MESH,
        )

    for j in range(heads):
        high = differences[j].astype(jnp.bfloat16)
        low = (differences[j] - high.astype(jnp.float32)).astype(jnp.bfloat16)
        grads[j] = rows_dot(features[j], high) + rows_dot(features[j], low)

        @pl.when(first_head + j != me)
        def _():
            grad_copy(j).start()

        @pl.when(first_head + j == me)
        def _():
            grads_in[z] = grads[j]

    for r in range(1, plane):
        share(losses, loss_send, loss_recv, r).wait_recv()
    mine = losses[0, pl.ds(pb, 1), :]
    for i in range(1, plane):
        mine = mine + losses[i, pl.ds(pb, 1), :]
    part = rows // nha
    chosen = mine[:, 0:part]
    for i in range(1, nha):
        chosen = jnp.where(ha == i, mine[:, i * part : (i + 1) * part], chosen)
    loss_ref[...] = chosen * (1.0 / (heads * plane * TD))

    giver_ha = me // (npb * heads)
    giver_pb = (me // heads) % npb
    for i in range(nkv):

        @pl.when((giver_ha != ha) | (giver_pb != pb) | (z != i))
        def _():
            pltpu.make_async_remote_copy(
                src_ref=grads.at[0],
                dst_ref=grads_in.at[i],
                send_sem=grad_send.at[0],
                recv_sem=grad_recv.at[i],
                device_id=(giver_pb, i, giver_ha),
                device_id_type=MESH,
            ).wait_recv()

    total = grads_in[0]
    for i in range(1, nkv):
        total = total + grads_in[i]
    grad_ref[...] = total * (1.0 / math.sqrt(tokens))

    for r in range(1, npb):
        kv_copy(r).wait_send()
        q_copy(r, 0).wait_send()
        q_copy(r, 1).wait_send()
    for h in range(nkv - 1):
        for c in range(npb):

            @pl.when((z - h >= 0) & (z < nkv - 1))
            def _():
                chain(h, c, True).wait_send()

            if c < npb - 1:

                @pl.when((z + h <= nkv - 1) & (z > 0))
                def _():
                    chain(h, c, False).wait_send()

    for r in range(1, plane):
        share(stats, stat_send, stat_recv, r).wait_send()
        share(losses, loss_send, loss_recv, r).wait_send()
    for j in range(heads):

        @pl.when(first_head + j != me)
        def _():
            grad_copy(j).wait_send()


def by_heads(
    shape, teacher_q, teacher_k, teacher_v, student_q, student_k, student_v, doc_ids, proj_weight
):
    npb, nkv, nha = shape
    rows = teacher_q.shape[0]
    heads = teacher_q.shape[1] // (npb * TD)
    wide = heads * rows
    plane = npb * nha
    dma = pltpu.SemaphoreType.DMA
    bf16, f32 = jnp.bfloat16, jnp.float32
    vmem = pl.BlockSpec(memory_space=pltpu.VMEM)
    grad, loss = pl.pallas_call(
        functools.partial(fused, shape, rows * npb * nkv),
        out_shape=(
            jax.ShapeDtypeStruct((SD, TD), f32),
            jax.ShapeDtypeStruct((1, rows // nha), f32),
        ),
        in_specs=[pl.BlockSpec(memory_space=pltpu.HBM)] * 8,
        out_specs=(vmem, vmem),
        scratch_shapes=[
            pltpu.VMEM(teacher_k.shape, bf16),
            pltpu.VMEM(teacher_v.shape, bf16),
            pltpu.VMEM(student_k.shape, bf16),
            pltpu.VMEM(student_v.shape, bf16),
            pltpu.VMEM((1, rows), jnp.int32),
            pltpu.VMEM((heads, SD, TD), bf16),
            pltpu.VMEM((npb, 3 * rows + 16, TD), bf16),
            pltpu.VMEM((nkv, npb, 3 * rows + 16, TD), bf16),
            pltpu.VMEM((npb, rows, heads * TD), bf16),
            pltpu.VMEM((npb, rows, heads * SD), bf16),
            pltpu.VMEM((npb, wide, TD), bf16),
            pltpu.VMEM((npb, wide, TD), bf16),
            pltpu.VMEM((npb, TD, wide), f32),
            pltpu.VMEM((npb, SD, wide), f32),
            pltpu.VMEM((npb, 8, wide), f32),
            pltpu.VMEM((plane, 8, rows), f32),
            pltpu.VMEM((plane, 8, rows), f32),
            pltpu.VMEM((heads, SD, TD), f32),
            pltpu.VMEM((nkv, SD, TD), f32),
            dma((npb,)),
            dma((npb,)),
            dma((npb, 2)),
            dma((npb, 2)),
            dma((nkv, npb)),
            dma((nkv, npb)),
            dma((nkv, npb)),
            dma((nkv, npb)),
            dma((plane,)),
            dma((plane,)),
            dma((plane,)),
            dma((plane,)),
            dma((heads,)),
            dma((nkv,)),
            dma((8,)),
        ],
        compiler_params=pltpu.CompilerParams(
            collective_id=0, has_side_effects=True, vmem_limit_bytes=63 * 1024 * 1024
        ),
        name="attention_distillation",
    )(
        teacher_q,
        teacher_k,
        teacher_v,
        student_q,
        student_k,
        student_v,
        doc_ids.reshape(1, rows),
        proj_weight,
    )
    return grad, loss.reshape(-1)


def local(*arguments):
    teacher_q, teacher_k, proj_weight = arguments[0], arguments[1], arguments[7]
    shape = tuple(lax.axis_size(name) for name in ("pb", "kv", "ha"))
    groups = teacher_k.shape[1] // TD
    fits = (
        groups == shape[0] == 4
        and shape[2] == 2
        and math.prod(shape) == proj_weight.shape[0]
        and teacher_q.shape[0] == 128
    )
    if fits:
        return by_heads(shape, *arguments)
    return gathered(*arguments)


def solution(mesh):
    in_specs = (
        P(("pb", "kv"), "ha"),
        P(("pb", "kv"), "ha"),
        P(("pb", "kv"), "ha"),
        P(("pb", "kv"), "ha"),
        P(("pb", "kv"), "ha"),
        P(("pb", "kv"), "ha"),
        P(("pb", "kv")),
        P(),
    )
    out_specs = (P(("pb", "kv", "ha"), None), P(("pb", "kv", "ha")))
    return jax.shard_map(local, mesh=mesh, in_specs=in_specs, out_specs=out_specs, check_vma=False)
```

```python
import functools
import math

import jax
import jax.numpy as jnp
from jax import lax
from jax.experimental import pallas as pl
from jax.experimental.pallas import tpu as pltpu
from jax.sharding import PartitionSpec as P

MESH = pl.DeviceIdType.MESH

TD = 128
SD = 64
DOCS = 4


NEGATIVE = -1e30
EPSILON = 1e-06


def start_state(queries, head_size, groups):
    queried = queries.shape[0]
    per_group = queries.shape[1] // (groups * head_size)
    largest = jnp.full((groups, per_group, queried), NEGATIVE, jnp.float32)
    totals = jnp.zeros((groups, per_group, queried), jnp.float32)
    accum = jnp.zeros((groups, per_group, queried, head_size), jnp.float32)
    return (largest, totals, accum)


def attend_keys(
    state, queries, query_pos, query_doc, keys_piece, values_piece, key_pos, key_doc, head_size
):
    length = keys_piece.shape[0]
    block = math.gcd(length, 512)
    blocks = length // block
    groups = keys_piece.shape[1] // head_size
    queried = queries.shape[0]
    per_group = queries.shape[1] // (groups * head_size)
    shaped = queries.reshape(queried, groups, per_group, head_size)
    scale = 1.0 / math.sqrt(head_size)
    newest = jnp.max(query_pos)

    def compute(current, key_block, value_block, pos_block, doc_block):
        largest, totals, accum = current
        scores = (
            jnp.einsum(
                "qgpd,kgd->gpqk",
                shaped,
                key_block.reshape(block, groups, head_size),
                preferred_element_type=jnp.float32,
            )
            * scale
        )
        allowed = (query_doc[:, None] == doc_block[None, :]) & (
            pos_block[None, :] <= query_pos[:, None]
        )
        scores = jnp.where(allowed, scores, NEGATIVE)
        updated = jnp.maximum(largest, jnp.max(scores, axis=-1))
        weights = jnp.where(allowed, jnp.exp(scores - updated[..., None]), 0.0)
        factor = jnp.exp(largest - updated)
        totals = totals * factor + jnp.sum(weights, axis=-1)
        mixed = jnp.einsum(
            "gpqk,kgd->gpqd",
            weights.astype(jnp.bfloat16),
            value_block.reshape(block, groups, head_size),
            preferred_element_type=jnp.float32,
        )
        return (updated, totals, accum * factor[..., None] + mixed)

    def visit(current, item):
        key_block, value_block, pos_block, doc_block = item
        result = lax.cond(
            pos_block[0] <= newest,
            lambda inner: compute(inner, key_block, value_block, pos_block, doc_block),
            lambda inner: inner,
            current,
        )
        return (result, None)

    items = (
        keys_piece.reshape(blocks, block, -1),
        values_piece.reshape(blocks, block, -1),
        key_pos.reshape(blocks, block),
        key_doc.reshape(blocks, block),
    )
    final, unused = lax.scan(visit, state, items)
    return final


def finish(totals, accum):
    queried = accum.shape[2]
    result = accum / totals[..., None]
    return jnp.transpose(result, (2, 0, 1, 3)).reshape(queried, -1).astype(jnp.bfloat16)


def gathered(teacher_q, teacher_k, teacher_v, student_q, student_k, student_v, doc_ids, proj_weight):
    shard_rows = teacher_q.shape[0]
    groups = teacher_k.shape[1] // TD
    outer = lax.axis_size("pb")
    inner_size = lax.axis_size("kv")
    total_tokens = shard_rows * outer * inner_size
    shard = lax.axis_index("pb") * inner_size + lax.axis_index("kv")
    own_pos = shard * shard_rows + jnp.arange(shard_rows, dtype=jnp.int32)
    initial = (start_state(teacher_q, TD, groups), start_state(student_q, SD, groups))
    key_teacher = lax.all_gather(teacher_k, ("pb", "kv"), axis=0, tiled=True)
    value_teacher = lax.all_gather(teacher_v, ("pb", "kv"), axis=0, tiled=True)
    key_student = lax.all_gather(student_k, ("pb", "kv"), axis=0, tiled=True)
    value_student = lax.all_gather(student_v, ("pb", "kv"), axis=0, tiled=True)
    piece_doc = lax.all_gather(doc_ids, ("pb", "kv"), axis=0, tiled=True)
    key_pos = jnp.arange(piece_doc.shape[0], dtype=jnp.int32)
    teacher_state = attend_keys(
        initial[0], teacher_q, own_pos, doc_ids, key_teacher, value_teacher, key_pos, piece_doc, TD
    )
    student_state = attend_keys(
        initial[1], student_q, own_pos, doc_ids, key_student, value_student, key_pos, piece_doc, SD
    )
    teacher_state, student_state = (teacher_state, student_state)
    teacher_out = finish(teacher_state[1], teacher_state[2])
    student_out = finish(student_state[1], student_state[2])
    teacher_half, student_half = (
        lax.all_to_all(teacher_out, "ha", split_axis=0, concat_axis=1, tiled=True),
        lax.all_to_all(student_out, "ha", split_axis=0, concat_axis=1, tiled=True),
    )
    count = teacher_half.shape[0]
    heads = proj_weight.shape[0]
    teacher_float = teacher_half.astype(jnp.float32)
    target = teacher_float * lax.rsqrt(
        jnp.mean(teacher_float * teacher_float, axis=1, keepdims=True) + EPSILON
    )
    student_float = student_half.astype(jnp.float32)
    features = (
        student_float
        * lax.rsqrt(jnp.mean(student_float * student_float, axis=1, keepdims=True) + EPSILON)
    ).astype(jnp.bfloat16)
    feature_heads = features.reshape(count, heads, -1)
    predicted = jnp.einsum(
        "thd,hde->the", feature_heads, proj_weight, preferred_element_type=jnp.float32
    )
    difference = predicted.reshape(count, -1) - target
    token_loss = jnp.mean(difference * difference, axis=1)
    gradient = jnp.einsum(
        "thd,the->hde",
        feature_heads.astype(jnp.float32),
        difference.reshape(count, heads, -1),
        precision=lax.Precision.HIGHEST,
    )
    gradient = (gradient / math.sqrt(total_tokens)).reshape(-1, gradient.shape[2])
    grad_w = lax.psum_scatter(gradient, ("pb", "kv", "ha"), scatter_dimension=0, tiled=True)
    return (grad_w, token_loss)

def rows_dot(a, b):
    return lax.dot_general(a, b, (((1,), (1,)), ((), ())), preferred_element_type=jnp.float32)


def columns_dot(a, b):
    return lax.dot_general(a, b, (((0,), (0,)), ((), ())), preferred_element_type=jnp.float32)


def fused(
    shape,
    tokens,
    tq_ref,
    tk_hbm,
    tv_hbm,
    sq_ref,
    sk_hbm,
    sv_hbm,
    doc_hbm,
    w_hbm,
    grad_ref,
    loss_ref,
    tk_ref,
    tv_ref,
    sk_ref,
    sv_ref,
    doc_ref,
    w_ref,
    stage,
    kv,
    tq_in,
    sq_in,
    tq_all,
    sq_all,
    t_acc,
    s_acc,
    soft,
    stats,
    losses,
    grads,
    grads_in,
    xy_send,
    xy_recv,
    q_send,
    q_recv,
    up_send,
    up_recv,
    down_send,
    down_recv,
    stat_send,
    stat_recv,
    loss_send,
    loss_recv,
    grad_send,
    grad_recv,
    load_sem,
):
    npb, nkv, nha = shape
    devices = npb * nkv * nha
    rows = tq_ref.shape[0]
    heads = tq_ref.shape[1] // (npb * TD)
    wide = heads * rows
    pb, z, ha = lax.axis_index("pb"), lax.axis_index("kv"), lax.axis_index("ha")
    me = (pb * nkv + z) * nha + ha

    def coords(index):
        return (index // (nkv * nha), (index // nha) % nkv, index % nha)

    first_head = (ha * npb + pb) * heads

    def query_part(place, which):
        ref, width = ((tq_ref, heads * TD), (sq_ref, heads * SD))[which]
        return ref.at[:, pl.ds(pl.multiple_of(place * width, width), width)]

    loads = [
        pltpu.make_async_copy(source, into, load_sem.at[i])
        for i, (source, into) in enumerate(
            (
                (tk_hbm, tk_ref),
                (tv_hbm, tv_ref),
                (sk_hbm, sk_ref),
                (sv_hbm, sv_ref),
                (doc_hbm, doc_ref),
                (w_hbm.at[pl.ds(first_head, heads)], w_ref),
                (query_part(pb, 0), tq_in.at[pb]),
                (query_part(pb, 1), sq_in.at[pb]),
            )
        )
    ]
    for load in loads:
        load.start()

    barrier = pltpu.get_barrier_semaphore()

    def greet(r, carry):
        pl.semaphore_signal(
            barrier, inc=1, device_id=coords((me + r) % devices), device_id_type=MESH
        )
        return carry

    lax.fori_loop(1, devices, greet, 0)

    for load in loads[:5]:
        load.wait()
    doc_rows = jnp.broadcast_to(doc_ref[...].astype(jnp.float32), (16, rows)).astype(jnp.bfloat16)
    for g in range(npb):
        stage[g, 0:rows, :] = tk_ref[:, g * TD : (g + 1) * TD]
        stage[g, rows : 2 * rows, :] = (
            tv_ref[:, g * TD : (g + 1) * TD].astype(jnp.float32).T.astype(jnp.bfloat16)
        )
        stage[g, 2 * rows : 3 * rows, :] = jnp.concatenate(
            [sk_ref[:, g * SD : (g + 1) * SD], sv_ref[:, g * SD : (g + 1) * SD]], axis=1
        )
        stage[g, 3 * rows : 3 * rows + 16, :] = doc_rows
    kv[z, pb] = stage[pb]

    pl.semaphore_wait(barrier, devices - 1)

    def partner(r):
        return ((pb // 2 + r // 2) % 2) * 2 + (pb % 2 + r % 2) % 2

    def kv_copy(r):
        to = partner(r)
        return pltpu.make_async_remote_copy(
            src_ref=stage.at[to],
            dst_ref=kv.at[z, pb],
            send_sem=xy_send.at[r],
            recv_sem=xy_recv.at[r],
            device_id=(to, z, ha),
            device_id_type=MESH,
        )

    def q_copy(r, which):
        to = partner(r)
        return pltpu.make_async_remote_copy(
            src_ref=query_part(to, which),
            dst_ref=(tq_in, sq_in)[which].at[pb],
            send_sem=q_send.at[r, which],
            recv_sem=q_recv.at[r, which],
            device_id=(to, z, ha),
            device_id_type=MESH,
        )

    for r in range(1, npb):
        kv_copy(r).start()

    def chain(h, c, up):
        piece = kv.at[z - h if up else z + h, c]
        send, recv = (up_send, up_recv) if up else (down_send, down_recv)
        return pltpu.make_async_remote_copy(
            src_ref=piece,
            dst_ref=piece,
            send_sem=send.at[h, c],
            recv_sem=recv.at[h, c],
            device_id=(pb, z + 1 if up else z - 1, ha),
            device_id_type=MESH,
        )

    def arrived(h, c, up):
        piece = kv.at[z - h if up else z + h, c]
        send, recv = (up_send, up_recv) if up else (down_send, down_recv)
        pltpu.make_async_remote_copy(
            src_ref=piece,
            dst_ref=piece,
            send_sem=send.at[h - 1, c],
            recv_sem=recv.at[h - 1, c],
            device_id=(pb, z - 1 if up else z + 1, ha),
            device_id_type=MESH,
        ).wait_recv()

    for r in range(npb):
        if r > 0:
            kv_copy(r).wait_recv()

        @pl.when(z < nkv - 1)
        def _():
            chain(0, partner(r), True).start()

        @pl.when((z > 0) & (partner(r) < npb - 1))
        def _():
            chain(0, partner(r), False).start()

    for r in range(1, npb):
        q_copy(r, 0).start()
        q_copy(r, 1).start()

    def next_hop(h, c):
        @pl.when(z - h >= 0)
        def _():
            arrived(h, c, True)

            @pl.when(z < nkv - 1)
            def _():
                chain(h, c, True).start()

        if not isinstance(c, int) or c < npb - 1:

            @pl.when((z + h <= nkv - 1) & (c < npb - 1))
            def _():
                arrived(h, c, False)

                @pl.when(z > 0)
                def _():
                    chain(h, c, False).start()

    t_acc[...] = jnp.zeros_like(t_acc)
    s_acc[...] = jnp.zeros_like(s_acc)
    soft[:, 0:2, :] = jnp.full((npb, 2, wide), NEGATIVE, jnp.float32)
    soft[:, 2:4, :] = jnp.zeros((npb, 2, wide), jnp.float32)

    local_key = lax.broadcasted_iota(jnp.int32, (rows, wide), 0)
    local_query = lax.broadcasted_iota(jnp.int32, (1, wide), 1) % rows
    float_key = local_key.astype(jnp.float32)
    float_query = local_query.astype(jnp.float32)

    def masked_scores(source, p, count, own_place):
        own = kv[z, p, 3 * rows : 3 * rows + 16, :].astype(jnp.float32)[0:1, :]
        query_doc = jnp.concatenate([own] * heads, axis=1)
        firsts = []
        for c in range(count):
            key_doc = kv[source, c, 3 * rows : 3 * rows + 16, :].astype(jnp.float32)[0:1, :]
            least = jnp.zeros((1, wide), jnp.float32)
            for d in range(1, DOCS):
                before = jnp.sum((key_doc < d).astype(jnp.float32), axis=1, keepdims=True)
                least = jnp.where(query_doc == d, before, least)
            firsts.append(least)

        def allowed(c, which):
            if which == 0:
                ok = local_key >= firsts[c].astype(jnp.int32)
                return ok & (local_key <= local_query) if own_place and c == p else ok
            ok = float_key > firsts[c] - 0.5
            return ok & (float_key < float_query + 0.5) if own_place and c == p else ok

        result = []
        for which in range(2):
            cut = slice(0, rows) if which == 0 else slice(2 * rows, 3 * rows)
            key_rows = kv[source, 0:count, cut, :].reshape(count * rows, TD)
            raw = rows_dot(key_rows, (tq_all, sq_all)[which][p])
            result.append(
                jnp.concatenate(
                    [
                        jnp.where(allowed(c, which), raw[c * rows : (c + 1) * rows], NEGATIVE)
                        for c in range(count)
                    ],
                    axis=0,
                )
            )
        return result

    def absorb(source, p, count, which, scores):
        factor = 1.0 / math.sqrt(TD) if which == 0 else 1.0
        old = soft[p, which : which + 1, :]
        new = jnp.maximum(old, jnp.max(scores, axis=0, keepdims=True))
        weights = jnp.exp((scores - new) * factor)
        shrink = jnp.exp((old - new) * factor)
        soft[p, which : which + 1, :] = new
        soft[p, which + 2 : which + 3, :] = soft[
            p, which + 2 : which + 3, :
        ] * shrink + jnp.sum(weights, axis=0, keepdims=True)
        rounded = weights.astype(jnp.bfloat16)
        if which == 0:
            values = jnp.concatenate(
                [kv[source, c, rows : 2 * rows, :] for c in range(count)], axis=1
            )
            t_acc[p] = t_acc[p] * shrink + jnp.dot(
                values, rounded, preferred_element_type=jnp.float32
            )
        else:
            key_rows = kv[source, 0:count, 2 * rows : 3 * rows, :].reshape(count * rows, TD)
            s_acc[p] = s_acc[p] * shrink + columns_dot(key_rows, rounded)[TD - SD :]

    def attend(source, pairs, own_place=False):
        scores = masked_scores(source, *pairs[0], own_place)
        for i, (p, count) in enumerate(pairs):
            later = None
            if i + 1 < len(pairs):
                later = masked_scores(source, *pairs[i + 1], own_place)
            for which in range(2):
                absorb(source, p, count, which, scores[which])
            scores = later

    for load in loads[5:]:
        load.wait()
    blank = jnp.zeros((rows, TD - SD), jnp.bfloat16)
    scale = jnp.asarray(1.0 / math.sqrt(SD), jnp.bfloat16)

    def own_turn(r, carry):
        place = partner(r)
        next_hop(1, place)

        @pl.when(r > 0)
        def _():
            q_copy(r, 0).wait_recv()
            q_copy(r, 1).wait_recv()

        for j in range(heads):
            tq_all[place, j * rows : (j + 1) * rows, :] = tq_in[place, :, j * TD : (j + 1) * TD]
            sq_all[place, j * rows : (j + 1) * rows, :] = jnp.concatenate(
                [sq_in[place, :, j * SD : (j + 1) * SD] * scale, blank], axis=1
            )
        for p in range(npb):

            @pl.when(place == p)
            def _():
                attend(z, [(p, p + 1)], True)

        return carry

    lax.fori_loop(0, npb, own_turn, 0)

    def hops(h, pieces):
        for c in pieces:

            @pl.when(h >= 2)
            def _():
                next_hop(h, c)

    def turn(h, carry):
        hops(h, range(npb - 1))

        @pl.when(z - h >= 0)
        def _():
            attend(z - h, [(p, p + 1) for p in range(npb - 1)])

        hops(h, range(npb - 1, npb))

        @pl.when(z - h >= 0)
        def _():
            attend(z - h, [(npb - 1, npb)])

        @pl.when(z + h <= nkv - 1)
        def _():
            attend(z + h, [(p, p) for p in range(1, npb)])

        return carry

    lax.fori_loop(1, nkv, turn, 0)

    def by_token(row):
        total = row[:, 0:rows]
        for j in range(1, heads):
            total = total + row[:, j * rows : (j + 1) * rows]
        return total

    t_sums, s_sums, t_outs, s_outs = [], [], [], []
    for p in range(npb):
        t_out = (t_acc[p] / soft[p, 2:3, :]).astype(jnp.bfloat16).astype(jnp.float32)
        s_out = (s_acc[p] / soft[p, 3:4, :]).astype(jnp.bfloat16).astype(jnp.float32)
        t_acc[p] = t_out
        s_acc[p] = s_out
        t_sums.append(by_token(jnp.sum(t_out * t_out, axis=0, keepdims=True)))
        s_sums.append(by_token(jnp.sum(s_out * s_out, axis=0, keepdims=True)))

    plane = npb * nha
    slot = pb * nha + ha

    def share(buffer, send, recv, r):
        to = (slot + r) % plane
        return pltpu.make_async_remote_copy(
            src_ref=buffer.at[slot],
            dst_ref=buffer.at[slot],
            send_sem=send.at[r],
            recv_sem=recv.at[r],
            device_id=(to // nha, z, to % nha),
            device_id_type=MESH,
        )

    stats[slot] = jnp.concatenate(t_sums + s_sums, axis=0)
    for r in range(1, plane):
        share(stats, stat_send, stat_recv, r).start()
    for r in range(1, plane):
        share(stats, stat_send, stat_recv, r).wait_recv()
    sums = stats[0]
    for i in range(1, plane):
        sums = sums + stats[i]
    t_scale = lax.rsqrt(sums[0:npb] * (1.0 / (heads * plane * TD)) + EPSILON)
    s_scale = lax.rsqrt(sums[npb : 2 * npb] * (1.0 / (heads * plane * SD)) + EPSILON)

    loss = jnp.zeros((1, npb * rows), jnp.float32)
    features, differences = [], []
    for j in range(heads):
        cut = slice(j * rows, (j + 1) * rows)
        target = jnp.concatenate(
            [t_acc[p, :, cut] * t_scale[p : p + 1] for p in range(npb)], axis=1
        )
        feature = jnp.concatenate(
            [s_acc[p, :, cut] * s_scale[p : p + 1] for p in range(npb)], axis=1
        ).astype(jnp.bfloat16)
        difference = columns_dot(w_ref[j], feature) - target
        loss = loss + jnp.sum(difference * difference, axis=0, keepdims=True)
        features.append(feature)
        differences.append(difference)
    losses[slot] = jnp.concatenate(
        [loss[:, p * rows : (p + 1) * rows] for p in range(npb)]
        + [jnp.zeros((8 - npb, rows), jnp.float32)],
        axis=0,
    )
    for r in range(1, plane):
        share(losses, loss_send, loss_recv, r).start()

    def grad_copy(j):
        return pltpu.make_async_remote_copy(
            src_ref=grads.at[j],
            dst_ref=grads_in.at[z],
            send_sem=grad_send.at[j],
            recv_sem=grad_recv.at[z],
            device_id=coords(first_head + j),
            device_id_type=MESH,
        )

    for j in range(heads):
        high = differences[j].astype(jnp.bfloat16)
        low = (differences[j] - high.astype(jnp.float32)).astype(jnp.bfloat16)
        grads[j] = rows_dot(features[j], high) + rows_dot(features[j], low)

        @pl.when(first_head + j != me)
        def _():
            grad_copy(j).start()

        @pl.when(first_head + j == me)
        def _():
            grads_in[z] = grads[j]

    for r in range(1, plane):
        share(losses, loss_send, loss_recv, r).wait_recv()
    mine = losses[0, pl.ds(pb, 1), :]
    for i in range(1, plane):
        mine = mine + losses[i, pl.ds(pb, 1), :]
    part = rows // nha
    chosen = mine[:, 0:part]
    for i in range(1, nha):
        chosen = jnp.where(ha == i, mine[:, i * part : (i + 1) * part], chosen)
    loss_ref[...] = chosen * (1.0 / (heads * plane * TD))

    giver_ha = me // (npb * heads)
    giver_pb = (me // heads) % npb
    for i in range(nkv):

        @pl.when((giver_ha != ha) | (giver_pb != pb) | (z != i))
        def _():
            pltpu.make_async_remote_copy(
                src_ref=grads.at[0],
                dst_ref=grads_in.at[i],
                send_sem=grad_send.at[0],
                recv_sem=grad_recv.at[i],
                device_id=(giver_pb, i, giver_ha),
                device_id_type=MESH,
            ).wait_recv()

    total = grads_in[0]
    for i in range(1, nkv):
        total = total + grads_in[i]
    grad_ref[...] = total * (1.0 / math.sqrt(tokens))

    for r in range(1, npb):
        kv_copy(r).wait_send()
        q_copy(r, 0).wait_send()
        q_copy(r, 1).wait_send()
    for h in range(nkv - 1):
        for c in range(npb):

            @pl.when((z - h >= 0) & (z < nkv - 1))
            def _():
                chain(h, c, True).wait_send()

            if c < npb - 1:

                @pl.when((z + h <= nkv - 1) & (z > 0))
                def _():
                    chain(h, c, False).wait_send()

    for r in range(1, plane):
        share(stats, stat_send, stat_recv, r).wait_send()
        share(losses, loss_send, loss_recv, r).wait_send()
    for j in range(heads):

        @pl.when(first_head + j != me)
        def _():
            grad_copy(j).wait_send()


def by_heads(
    shape, teacher_q, teacher_k, teacher_v, student_q, student_k, student_v, doc_ids, proj_weight
):
    npb, nkv, nha = shape
    rows = teacher_q.shape[0]
    heads = teacher_q.shape[1] // (npb * TD)
    wide = heads * rows
    plane = npb * nha
    dma = pltpu.SemaphoreType.DMA
    bf16, f32 = jnp.bfloat16, jnp.float32
    vmem = pl.BlockSpec(memory_space=pltpu.VMEM)
    grad, loss = pl.pallas_call(
        functools.partial(fused, shape, rows * npb * nkv),
        out_shape=(
            jax.ShapeDtypeStruct((SD, TD), f32),
            jax.ShapeDtypeStruct((1, rows // nha), f32),
        ),
        in_specs=[pl.BlockSpec(memory_space=pltpu.HBM)] * 8,
        out_specs=(vmem, vmem),
        scratch_shapes=[
            pltpu.VMEM(teacher_k.shape, bf16),
            pltpu.VMEM(teacher_v.shape, bf16),
            pltpu.VMEM(student_k.shape, bf16),
            pltpu.VMEM(student_v.shape, bf16),
            pltpu.VMEM((1, rows), jnp.int32),
            pltpu.VMEM((heads, SD, TD), bf16),
            pltpu.VMEM((npb, 3 * rows + 16, TD), bf16),
            pltpu.VMEM((nkv, npb, 3 * rows + 16, TD), bf16),
            pltpu.VMEM((npb, rows, heads * TD), bf16),
            pltpu.VMEM((npb, rows, heads * SD), bf16),
            pltpu.VMEM((npb, wide, TD), bf16),
            pltpu.VMEM((npb, wide, TD), bf16),
            pltpu.VMEM((npb, TD, wide), f32),
            pltpu.VMEM((npb, SD, wide), f32),
            pltpu.VMEM((npb, 8, wide), f32),
            pltpu.VMEM((plane, 8, rows), f32),
            pltpu.VMEM((plane, 8, rows), f32),
            pltpu.VMEM((heads, SD, TD), f32),
            pltpu.VMEM((nkv, SD, TD), f32),
            dma((npb,)),
            dma((npb,)),
            dma((npb, 2)),
            dma((npb, 2)),
            dma((nkv, npb)),
            dma((nkv, npb)),
            dma((nkv, npb)),
            dma((nkv, npb)),
            dma((plane,)),
            dma((plane,)),
            dma((plane,)),
            dma((plane,)),
            dma((heads,)),
            dma((nkv,)),
            dma((8,)),
        ],
        compiler_params=pltpu.CompilerParams(
            collective_id=0, has_side_effects=True, vmem_limit_bytes=63 * 1024 * 1024
        ),
        name="attention_distillation",
    )(
        teacher_q,
        teacher_k,
        teacher_v,
        student_q,
        student_k,
        student_v,
        doc_ids.reshape(1, rows),
        proj_weight,
    )
    return grad, loss.reshape(-1)


def local(*arguments):
    teacher_q, teacher_k, proj_weight = arguments[0], arguments[1], arguments[7]
    shape = tuple(lax.axis_size(name) for name in ("pb", "kv", "ha"))
    groups = teacher_k.shape[1] // TD
    fits = (
        groups == shape[0] == 4
        and shape[2] == 2
        and math.prod(shape) == proj_weight.shape[0]
        and teacher_q.shape[0] == 128
    )
    if fits:
        return by_heads(shape, *arguments)
    return gathered(*arguments)


def solution(mesh):
    in_specs = (
        P(("pb", "kv"), "ha"),
        P(("pb", "kv"), "ha"),
        P(("pb", "kv"), "ha"),
        P(("pb", "kv"), "ha"),
        P(("pb", "kv"), "ha"),
        P(("pb", "kv"), "ha"),
        P(("pb", "kv")),
        P(),
    )
    out_specs = (P(("pb", "kv", "ha"), None), P(("pb", "kv", "ha")))
    return jax.shard_map(local, mesh=mesh, in_specs=in_specs, out_specs=out_specs, check_vma=False)
```

```python
import functools
import math

import jax
import jax.numpy as jnp
from jax import lax
from jax.experimental import pallas as pl
from jax.experimental.pallas import tpu as pltpu
from jax.sharding import PartitionSpec as P

MESH = pl.DeviceIdType.MESH

TD = 128
SD = 64
DOCS = 4


NEGATIVE = -1e30
EPSILON = 1e-06


def start_state(queries, head_size, groups):
    queried = queries.shape[0]
    per_group = queries.shape[1] // (groups * head_size)
    largest = jnp.full((groups, per_group, queried), NEGATIVE, jnp.float32)
    totals = jnp.zeros((groups, per_group, queried), jnp.float32)
    accum = jnp.zeros((groups, per_group, queried, head_size), jnp.float32)
    return (largest, totals, accum)


def attend_keys(
    state, queries, query_pos, query_doc, keys_piece, values_piece, key_pos, key_doc, head_size
):
    length = keys_piece.shape[0]
    block = math.gcd(length, 512)
    blocks = length // block
    groups = keys_piece.shape[1] // head_size
    queried = queries.shape[0]
    per_group = queries.shape[1] // (groups * head_size)
    shaped = queries.reshape(queried, groups, per_group, head_size)
    scale = 1.0 / math.sqrt(head_size)
    newest = jnp.max(query_pos)

    def compute(current, key_block, value_block, pos_block, doc_block):
        largest, totals, accum = current
        scores = (
            jnp.einsum(
                "qgpd,kgd->gpqk",
                shaped,
                key_block.reshape(block, groups, head_size),
                preferred_element_type=jnp.float32,
            )
            * scale
        )
        allowed = (query_doc[:, None] == doc_block[None, :]) & (
            pos_block[None, :] <= query_pos[:, None]
        )
        scores = jnp.where(allowed, scores, NEGATIVE)
        updated = jnp.maximum(largest, jnp.max(scores, axis=-1))
        weights = jnp.where(allowed, jnp.exp(scores - updated[..., None]), 0.0)
        factor = jnp.exp(largest - updated)
        totals = totals * factor + jnp.sum(weights, axis=-1)
        mixed = jnp.einsum(
            "gpqk,kgd->gpqd",
            weights.astype(jnp.bfloat16),
            value_block.reshape(block, groups, head_size),
            preferred_element_type=jnp.float32,
        )
        return (updated, totals, accum * factor[..., None] + mixed)

    def visit(current, item):
        key_block, value_block, pos_block, doc_block = item
        result = lax.cond(
            pos_block[0] <= newest,
            lambda inner: compute(inner, key_block, value_block, pos_block, doc_block),
            lambda inner: inner,
            current,
        )
        return (result, None)

    items = (
        keys_piece.reshape(blocks, block, -1),
        values_piece.reshape(blocks, block, -1),
        key_pos.reshape(blocks, block),
        key_doc.reshape(blocks, block),
    )
    final, unused = lax.scan(visit, state, items)
    return final


def finish(totals, accum):
    queried = accum.shape[2]
    result = accum / totals[..., None]
    return jnp.transpose(result, (2, 0, 1, 3)).reshape(queried, -1).astype(jnp.bfloat16)


def gathered(teacher_q, teacher_k, teacher_v, student_q, student_k, student_v, doc_ids, proj_weight):
    shard_rows = teacher_q.shape[0]
    groups = teacher_k.shape[1] // TD
    outer = lax.axis_size("pb")
    inner_size = lax.axis_size("kv")
    total_tokens = shard_rows * outer * inner_size
    shard = lax.axis_index("pb") * inner_size + lax.axis_index("kv")
    own_pos = shard * shard_rows + jnp.arange(shard_rows, dtype=jnp.int32)
    initial = (start_state(teacher_q, TD, groups), start_state(student_q, SD, groups))
    key_teacher = lax.all_gather(teacher_k, ("pb", "kv"), axis=0, tiled=True)
    value_teacher = lax.all_gather(teacher_v, ("pb", "kv"), axis=0, tiled=True)
    key_student = lax.all_gather(student_k, ("pb", "kv"), axis=0, tiled=True)
    value_student = lax.all_gather(student_v, ("pb", "kv"), axis=0, tiled=True)
    piece_doc = lax.all_gather(doc_ids, ("pb", "kv"), axis=0, tiled=True)
    key_pos = jnp.arange(piece_doc.shape[0], dtype=jnp.int32)
    teacher_state = attend_keys(
        initial[0], teacher_q, own_pos, doc_ids, key_teacher, value_teacher, key_pos, piece_doc, TD
    )
    student_state = attend_keys(
        initial[1], student_q, own_pos, doc_ids, key_student, value_student, key_pos, piece_doc, SD
    )
    teacher_state, student_state = (teacher_state, student_state)
    teacher_out = finish(teacher_state[1], teacher_state[2])
    student_out = finish(student_state[1], student_state[2])
    teacher_half, student_half = (
        lax.all_to_all(teacher_out, "ha", split_axis=0, concat_axis=1, tiled=True),
        lax.all_to_all(student_out, "ha", split_axis=0, concat_axis=1, tiled=True),
    )
    count = teacher_half.shape[0]
    heads = proj_weight.shape[0]
    teacher_float = teacher_half.astype(jnp.float32)
    target = teacher_float * lax.rsqrt(
        jnp.mean(teacher_float * teacher_float, axis=1, keepdims=True) + EPSILON
    )
    student_float = student_half.astype(jnp.float32)
    features = (
        student_float
        * lax.rsqrt(jnp.mean(student_float * student_float, axis=1, keepdims=True) + EPSILON)
    ).astype(jnp.bfloat16)
    feature_heads = features.reshape(count, heads, -1)
    predicted = jnp.einsum(
        "thd,hde->the", feature_heads, proj_weight, preferred_element_type=jnp.float32
    )
    difference = predicted.reshape(count, -1) - target
    token_loss = jnp.mean(difference * difference, axis=1)
    gradient = jnp.einsum(
        "thd,the->hde",
        feature_heads.astype(jnp.float32),
        difference.reshape(count, heads, -1),
        precision=lax.Precision.HIGHEST,
    )
    gradient = (gradient / math.sqrt(total_tokens)).reshape(-1, gradient.shape[2])
    grad_w = lax.psum_scatter(gradient, ("pb", "kv", "ha"), scatter_dimension=0, tiled=True)
    return (grad_w, token_loss)

def rows_dot(a, b):
    return lax.dot_general(a, b, (((1,), (1,)), ((), ())), preferred_element_type=jnp.float32)


def columns_dot(a, b):
    return lax.dot_general(a, b, (((0,), (0,)), ((), ())), preferred_element_type=jnp.float32)


def fused(
    shape,
    tokens,
    tq_ref,
    tk_hbm,
    tv_hbm,
    sq_ref,
    sk_hbm,
    sv_hbm,
    doc_hbm,
    w_hbm,
    grad_ref,
    loss_ref,
    tk_ref,
    tv_ref,
    sk_ref,
    sv_ref,
    doc_ref,
    w_ref,
    stage,
    kv,
    tq_in,
    sq_in,
    tq_all,
    sq_all,
    t_acc,
    s_acc,
    soft,
    stats,
    losses,
    grads,
    grads_in,
    xy_send,
    xy_recv,
    q_send,
    q_recv,
    up_send,
    up_recv,
    down_send,
    down_recv,
    stat_send,
    stat_recv,
    loss_send,
    loss_recv,
    grad_send,
    grad_recv,
    load_sem,
):
    npb, nkv, nha = shape
    devices = npb * nkv * nha
    rows = tq_ref.shape[0]
    heads = tq_ref.shape[1] // (npb * TD)
    wide = heads * rows
    pb, z, ha = lax.axis_index("pb"), lax.axis_index("kv"), lax.axis_index("ha")
    me = (pb * nkv + z) * nha + ha

    def coords(index):
        return (index // (nkv * nha), (index // nha) % nkv, index % nha)

    first_head = (ha * npb + pb) * heads

    def query_part(place, which):
        ref, width = ((tq_ref, heads * TD), (sq_ref, heads * SD))[which]
        return ref.at[:, pl.ds(pl.multiple_of(place * width, width), width)]

    loads = [
        pltpu.make_async_copy(source, into, load_sem.at[i])
        for i, (source, into) in enumerate(
            (
                (tk_hbm, tk_ref),
                (tv_hbm, tv_ref),
                (sk_hbm, sk_ref),
                (sv_hbm, sv_ref),
                (doc_hbm, doc_ref),
                (w_hbm.at[pl.ds(first_head, heads)], w_ref),
                (query_part(pb, 0), tq_in.at[pb]),
                (query_part(pb, 1), sq_in.at[pb]),
            )
        )
    ]
    for load in loads:
        load.start()

    barrier = pltpu.get_barrier_semaphore()

    def greet(r, carry):
        pl.semaphore_signal(
            barrier, inc=1, device_id=coords((me + r) % devices), device_id_type=MESH
        )
        return carry

    lax.fori_loop(1, devices, greet, 0)

    for load in loads[:5]:
        load.wait()
    doc_rows = jnp.broadcast_to(doc_ref[...].astype(jnp.float32), (16, rows)).astype(jnp.bfloat16)
    for g in range(npb):
        stage[g, 0:rows, :] = tk_ref[:, g * TD : (g + 1) * TD]
        stage[g, rows : 2 * rows, :] = (
            tv_ref[:, g * TD : (g + 1) * TD].astype(jnp.float32).T.astype(jnp.bfloat16)
        )
        stage[g, 2 * rows : 3 * rows, :] = jnp.concatenate(
            [sk_ref[:, g * SD : (g + 1) * SD], sv_ref[:, g * SD : (g + 1) * SD]], axis=1
        )
        stage[g, 3 * rows : 3 * rows + 16, :] = doc_rows
    kv[z, pb] = stage[pb]

    pl.semaphore_wait(barrier, devices - 1)

    def partner(r):
        return ((pb // 2 + r // 2) % 2) * 2 + (pb % 2 + r % 2) % 2

    def kv_copy(r):
        to = partner(r)
        return pltpu.make_async_remote_copy(
            src_ref=stage.at[to],
            dst_ref=kv.at[z, pb],
            send_sem=xy_send.at[r],
            recv_sem=xy_recv.at[r],
            device_id=(to, z, ha),
            device_id_type=MESH,
        )

    def q_copy(r, which):
        to = partner(r)
        return pltpu.make_async_remote_copy(
            src_ref=query_part(to, which),
            dst_ref=(tq_in, sq_in)[which].at[pb],
            send_sem=q_send.at[r, which],
            recv_sem=q_recv.at[r, which],
            device_id=(to, z, ha),
            device_id_type=MESH,
        )

    for r in range(1, npb):
        kv_copy(r).start()

    def chain(h, c, up):
        piece = kv.at[z - h if up else z + h, c]
        send, recv = (up_send, up_recv) if up else (down_send, down_recv)
        return pltpu.make_async_remote_copy(
            src_ref=piece,
            dst_ref=piece,
            send_sem=send.at[h, c],
            recv_sem=recv.at[h, c],
            device_id=(pb, z + 1 if up else z - 1, ha),
            device_id_type=MESH,
        )

    def arrived(h, c, up):
        piece = kv.at[z - h if up else z + h, c]
        send, recv = (up_send, up_recv) if up else (down_send, down_recv)
        pltpu.make_async_remote_copy(
            src_ref=piece,
            dst_ref=piece,
            send_sem=send.at[h - 1, c],
            recv_sem=recv.at[h - 1, c],
            device_id=(pb, z - 1 if up else z + 1, ha),
            device_id_type=MESH,
        ).wait_recv()

    for r in range(npb):
        if r > 0:
            kv_copy(r).wait_recv()

        @pl.when(z < nkv - 1)
        def _():
            chain(0, partner(r), True).start()

        @pl.when((z > 0) & (partner(r) < npb - 1))
        def _():
            chain(0, partner(r), False).start()

    for r in range(1, npb):
        q_copy(r, 0).start()
        q_copy(r, 1).start()

    def next_hop(h, c):
        @pl.when(z - h >= 0)
        def _():
            arrived(h, c, True)

            @pl.when(z < nkv - 1)
            def _():
                chain(h, c, True).start()

        if not isinstance(c, int) or c < npb - 1:

            @pl.when((z + h <= nkv - 1) & (c < npb - 1))
            def _():
                arrived(h, c, False)

                @pl.when(z > 0)
                def _():
                    chain(h, c, False).start()

    t_acc[...] = jnp.zeros_like(t_acc)
    s_acc[...] = jnp.zeros_like(s_acc)
    soft[:, 0:2, :] = jnp.full((npb, 2, wide), NEGATIVE, jnp.float32)
    soft[:, 2:4, :] = jnp.zeros((npb, 2, wide), jnp.float32)

    local_key = lax.broadcasted_iota(jnp.int32, (rows, wide), 0)
    local_query = lax.broadcasted_iota(jnp.int32, (1, wide), 1) % rows
    float_key = local_key.astype(jnp.float32)
    float_query = local_query.astype(jnp.float32)

    def masked_scores(source, p, count, own_place):
        own = kv[z, p, 3 * rows : 3 * rows + 16, :].astype(jnp.float32)[0:1, :]
        query_doc = jnp.concatenate([own] * heads, axis=1)
        firsts = []
        for c in range(count):
            key_doc = kv[source, c, 3 * rows : 3 * rows + 16, :].astype(jnp.float32)[0:1, :]
            least = jnp.zeros((1, wide), jnp.float32)
            for d in range(1, DOCS):
                before = jnp.sum((key_doc < d).astype(jnp.float32), axis=1, keepdims=True)
                least = jnp.where(query_doc == d, before, least)
            firsts.append(least)

        def allowed(c, which):
            if which == 0:
                ok = local_key >= firsts[c].astype(jnp.int32)
                return ok & (local_key <= local_query) if own_place and c == p else ok
            ok = float_key > firsts[c] - 0.5
            return ok & (float_key < float_query + 0.5) if own_place and c == p else ok

        result = []
        for which in range(2):
            cut = slice(0, rows) if which == 0 else slice(2 * rows, 3 * rows)
            key_rows = kv[source, 0:count, cut, :].reshape(count * rows, TD)
            raw = rows_dot(key_rows, (tq_all, sq_all)[which][p])
            result.append(
                jnp.concatenate(
                    [
                        jnp.where(allowed(c, which), raw[c * rows : (c + 1) * rows], NEGATIVE)
                        for c in range(count)
                    ],
                    axis=0,
                )
            )
        return result

    def absorb(source, p, count, which, scores):
        factor = 1.0 / math.sqrt(TD) if which == 0 else 1.0
        old = soft[p, which : which + 1, :]
        new = jnp.maximum(old, jnp.max(scores, axis=0, keepdims=True))
        weights = jnp.exp((scores - new) * factor)
        shrink = jnp.exp((old - new) * factor)
        soft[p, which : which + 1, :] = new
        soft[p, which + 2 : which + 3, :] = soft[
            p, which + 2 : which + 3, :
        ] * shrink + jnp.sum(weights, axis=0, keepdims=True)
        rounded = weights.astype(jnp.bfloat16)
        if which == 0:
            values = jnp.concatenate(
                [kv[source, c, rows : 2 * rows, :] for c in range(count)], axis=1
            )
            t_acc[p] = t_acc[p] * shrink + jnp.dot(
                values, rounded, preferred_element_type=jnp.float32
            )
        else:
            key_rows = kv[source, 0:count, 2 * rows : 3 * rows, :].reshape(count * rows, TD)
            s_acc[p] = s_acc[p] * shrink + columns_dot(key_rows, rounded)[TD - SD :]

    def attend(source, pairs, own_place=False):
        scores = masked_scores(source, *pairs[0], own_place)
        for i, (p, count) in enumerate(pairs):
            later = None
            if i + 1 < len(pairs):
                later = masked_scores(source, *pairs[i + 1], own_place)
            for which in range(2):
                absorb(source, p, count, which, scores[which])
            scores = later

    for load in loads[5:]:
        load.wait()
    blank = jnp.zeros((rows, TD - SD), jnp.bfloat16)
    scale = jnp.asarray(1.0 / math.sqrt(SD), jnp.bfloat16)

    def own_turn(r, carry):
        place = partner(r)

        @pl.when(r > 0)
        def _():
            q_copy(r, 0).wait_recv()
            q_copy(r, 1).wait_recv()

        for j in range(heads):
            tq_all[place, j * rows : (j + 1) * rows, :] = tq_in[place, :, j * TD : (j + 1) * TD]
            sq_all[place, j * rows : (j + 1) * rows, :] = jnp.concatenate(
                [sq_in[place, :, j * SD : (j + 1) * SD] * scale, blank], axis=1
            )
        for p in range(npb):

            @pl.when(place == p)
            def _():
                attend(z, [(p, p + 1)], True)

        next_hop(1, place)
        return carry

    lax.fori_loop(0, npb, own_turn, 0)

    def hops(h, early, pieces):
        for c in pieces:

            @pl.when(((h >= 2) & (h <= nkv - 2)) if early else (h == nkv - 1))
            def _():
                next_hop(h, c)

    def turn(h, carry):
        hops(h + 1, True, range(1))
        hops(h, False, range(npb - 1))

        @pl.when(z - h >= 0)
        def _():
            attend(z - h, [(p, p + 1) for p in range(npb - 1)])

        hops(h + 1, True, range(1, npb - 1))
        hops(h, False, range(npb - 1, npb))

        @pl.when(z - h >= 0)
        def _():
            attend(z - h, [(npb - 1, npb)])

        hops(h + 1, True, range(npb - 1, npb))

        @pl.when(z + h <= nkv - 1)
        def _():
            attend(z + h, [(p, p) for p in range(1, npb)])

        return carry

    lax.fori_loop(1, nkv, turn, 0)

    def by_token(row):
        total = row[:, 0:rows]
        for j in range(1, heads):
            total = total + row[:, j * rows : (j + 1) * rows]
        return total

    t_sums, s_sums, t_outs, s_outs = [], [], [], []
    for p in range(npb):
        t_out = (t_acc[p] / soft[p, 2:3, :]).astype(jnp.bfloat16).astype(jnp.float32)
        s_out = (s_acc[p] / soft[p, 3:4, :]).astype(jnp.bfloat16).astype(jnp.float32)
        t_acc[p] = t_out
        s_acc[p] = s_out
        t_sums.append(by_token(jnp.sum(t_out * t_out, axis=0, keepdims=True)))
        s_sums.append(by_token(jnp.sum(s_out * s_out, axis=0, keepdims=True)))

    plane = npb * nha
    slot = pb * nha + ha

    def share(buffer, send, recv, r):
        to = (slot + r) % plane
        return pltpu.make_async_remote_copy(
            src_ref=buffer.at[slot],
            dst_ref=buffer.at[slot],
            send_sem=send.at[r],
            recv_sem=recv.at[r],
            device_id=(to // nha, z, to % nha),
            device_id_type=MESH,
        )

    stats[slot] = jnp.concatenate(t_sums + s_sums, axis=0)
    for r in range(1, plane):
        share(stats, stat_send, stat_recv, r).start()
    for r in range(1, plane):
        share(stats, stat_send, stat_recv, r).wait_recv()
    sums = stats[0]
    for i in range(1, plane):
        sums = sums + stats[i]
    t_scale = lax.rsqrt(sums[0:npb] * (1.0 / (heads * plane * TD)) + EPSILON)
    s_scale = lax.rsqrt(sums[npb : 2 * npb] * (1.0 / (heads * plane * SD)) + EPSILON)

    loss = jnp.zeros((1, npb * rows), jnp.float32)
    features, differences = [], []
    for j in range(heads):
        cut = slice(j * rows, (j + 1) * rows)
        target = jnp.concatenate(
            [t_acc[p, :, cut] * t_scale[p : p + 1] for p in range(npb)], axis=1
        )
        feature = jnp.concatenate(
            [s_acc[p, :, cut] * s_scale[p : p + 1] for p in range(npb)], axis=1
        ).astype(jnp.bfloat16)
        difference = columns_dot(w_ref[j], feature) - target
        loss = loss + jnp.sum(difference * difference, axis=0, keepdims=True)
        features.append(feature)
        differences.append(difference)
    losses[slot] = jnp.concatenate(
        [loss[:, p * rows : (p + 1) * rows] for p in range(npb)]
        + [jnp.zeros((8 - npb, rows), jnp.float32)],
        axis=0,
    )
    for r in range(1, plane):
        share(losses, loss_send, loss_recv, r).start()

    def grad_copy(j):
        return pltpu.make_async_remote_copy(
            src_ref=grads.at[j],
            dst_ref=grads_in.at[z],
            send_sem=grad_send.at[j],
            recv_sem=grad_recv.at[z],
            device_id=coords(first_head + j),
            device_id_type=MESH,
        )

    for j in range(heads):
        high = differences[j].astype(jnp.bfloat16)
        low = (differences[j] - high.astype(jnp.float32)).astype(jnp.bfloat16)
        grads[j] = rows_dot(features[j], high) + rows_dot(features[j], low)

        @pl.when(first_head + j != me)
        def _():
            grad_copy(j).start()

        @pl.when(first_head + j == me)
        def _():
            grads_in[z] = grads[j]

    for r in range(1, plane):
        share(losses, loss_send, loss_recv, r).wait_recv()
    mine = losses[0, pl.ds(pb, 1), :]
    for i in range(1, plane):
        mine = mine + losses[i, pl.ds(pb, 1), :]
    part = rows // nha
    chosen = mine[:, 0:part]
    for i in range(1, nha):
        chosen = jnp.where(ha == i, mine[:, i * part : (i + 1) * part], chosen)
    loss_ref[...] = chosen * (1.0 / (heads * plane * TD))

    giver_ha = me // (npb * heads)
    giver_pb = (me // heads) % npb
    for i in range(nkv):

        @pl.when((giver_ha != ha) | (giver_pb != pb) | (z != i))
        def _():
            pltpu.make_async_remote_copy(
                src_ref=grads.at[0],
                dst_ref=grads_in.at[i],
                send_sem=grad_send.at[0],
                recv_sem=grad_recv.at[i],
                device_id=(giver_pb, i, giver_ha),
                device_id_type=MESH,
            ).wait_recv()

    total = grads_in[0]
    for i in range(1, nkv):
        total = total + grads_in[i]
    grad_ref[...] = total * (1.0 / math.sqrt(tokens))

    for r in range(1, npb):
        kv_copy(r).wait_send()
        q_copy(r, 0).wait_send()
        q_copy(r, 1).wait_send()
    for h in range(nkv - 1):
        for c in range(npb):

            @pl.when((z - h >= 0) & (z < nkv - 1))
            def _():
                chain(h, c, True).wait_send()

            if c < npb - 1:

                @pl.when((z + h <= nkv - 1) & (z > 0))
                def _():
                    chain(h, c, False).wait_send()

    for r in range(1, plane):
        share(stats, stat_send, stat_recv, r).wait_send()
        share(losses, loss_send, loss_recv, r).wait_send()
    for j in range(heads):

        @pl.when(first_head + j != me)
        def _():
            grad_copy(j).wait_send()


def by_heads(
    shape, teacher_q, teacher_k, teacher_v, student_q, student_k, student_v, doc_ids, proj_weight
):
    npb, nkv, nha = shape
    rows = teacher_q.shape[0]
    heads = teacher_q.shape[1] // (npb * TD)
    wide = heads * rows
    plane = npb * nha
    dma = pltpu.SemaphoreType.DMA
    bf16, f32 = jnp.bfloat16, jnp.float32
    vmem = pl.BlockSpec(memory_space=pltpu.VMEM)
    grad, loss = pl.pallas_call(
        functools.partial(fused, shape, rows * npb * nkv),
        out_shape=(
            jax.ShapeDtypeStruct((SD, TD), f32),
            jax.ShapeDtypeStruct((1, rows // nha), f32),
        ),
        in_specs=[pl.BlockSpec(memory_space=pltpu.HBM)] * 8,
        out_specs=(vmem, vmem),
        scratch_shapes=[
            pltpu.VMEM(teacher_k.shape, bf16),
            pltpu.VMEM(teacher_v.shape, bf16),
            pltpu.VMEM(student_k.shape, bf16),
            pltpu.VMEM(student_v.shape, bf16),
            pltpu.VMEM((1, rows), jnp.int32),
            pltpu.VMEM((heads, SD, TD), bf16),
            pltpu.VMEM((npb, 3 * rows + 16, TD), bf16),
            pltpu.VMEM((nkv, npb, 3 * rows + 16, TD), bf16),
            pltpu.VMEM((npb, rows, heads * TD), bf16),
            pltpu.VMEM((npb, rows, heads * SD), bf16),
            pltpu.VMEM((npb, wide, TD), bf16),
            pltpu.VMEM((npb, wide, TD), bf16),
            pltpu.VMEM((npb, TD, wide), f32),
            pltpu.VMEM((npb, SD, wide), f32),
            pltpu.VMEM((npb, 8, wide), f32),
            pltpu.VMEM((plane, 8, rows), f32),
            pltpu.VMEM((plane, 8, rows), f32),
            pltpu.VMEM((heads, SD, TD), f32),
            pltpu.VMEM((nkv, SD, TD), f32),
            dma((npb,)),
            dma((npb,)),
            dma((npb, 2)),
            dma((npb, 2)),
            dma((nkv, npb)),
            dma((nkv, npb)),
            dma((nkv, npb)),
            dma((nkv, npb)),
            dma((plane,)),
            dma((plane,)),
            dma((plane,)),
            dma((plane,)),
            dma((heads,)),
            dma((nkv,)),
            dma((8,)),
        ],
        compiler_params=pltpu.CompilerParams(
            collective_id=0, has_side_effects=True, vmem_limit_bytes=63 * 1024 * 1024
        ),
        name="attention_distillation",
    )(
        teacher_q,
        teacher_k,
        teacher_v,
        student_q,
        student_k,
        student_v,
        doc_ids.reshape(1, rows),
        proj_weight,
    )
    return grad, loss.reshape(-1)


def local(*arguments):
    teacher_q, teacher_k, proj_weight = arguments[0], arguments[1], arguments[7]
    shape = tuple(lax.axis_size(name) for name in ("pb", "kv", "ha"))
    groups = teacher_k.shape[1] // TD
    fits = (
        groups == shape[0] == 4
        and shape[2] == 2
        and math.prod(shape) == proj_weight.shape[0]
        and teacher_q.shape[0] == 128
    )
    if fits:
        return by_heads(shape, *arguments)
    return gathered(*arguments)


def solution(mesh):
    in_specs = (
        P(("pb", "kv"), "ha"),
        P(("pb", "kv"), "ha"),
        P(("pb", "kv"), "ha"),
        P(("pb", "kv"), "ha"),
        P(("pb", "kv"), "ha"),
        P(("pb", "kv"), "ha"),
        P(("pb", "kv")),
        P(),
    )
    out_specs = (P(("pb", "kv", "ha"), None), P(("pb", "kv", "ha")))
    return jax.shard_map(local, mesh=mesh, in_specs=in_specs, out_specs=out_specs, check_vma=False)
```

```python
import functools
import math

import jax
import jax.numpy as jnp
from jax import lax
from jax.experimental import pallas as pl
from jax.experimental.pallas import tpu as pltpu
from jax.sharding import PartitionSpec as P

MESH = pl.DeviceIdType.MESH

TD = 128
SD = 64
DOCS = 4


NEGATIVE = -1e30
EPSILON = 1e-06


def start_state(queries, head_size, groups):
    queried = queries.shape[0]
    per_group = queries.shape[1] // (groups * head_size)
    largest = jnp.full((groups, per_group, queried), NEGATIVE, jnp.float32)
    totals = jnp.zeros((groups, per_group, queried), jnp.float32)
    accum = jnp.zeros((groups, per_group, queried, head_size), jnp.float32)
    return (largest, totals, accum)


def attend_keys(
    state, queries, query_pos, query_doc, keys_piece, values_piece, key_pos, key_doc, head_size
):
    length = keys_piece.shape[0]
    block = math.gcd(length, 512)
    blocks = length // block
    groups = keys_piece.shape[1] // head_size
    queried = queries.shape[0]
    per_group = queries.shape[1] // (groups * head_size)
    shaped = queries.reshape(queried, groups, per_group, head_size)
    scale = 1.0 / math.sqrt(head_size)
    newest = jnp.max(query_pos)

    def compute(current, key_block, value_block, pos_block, doc_block):
        largest, totals, accum = current
        scores = (
            jnp.einsum(
                "qgpd,kgd->gpqk",
                shaped,
                key_block.reshape(block, groups, head_size),
                preferred_element_type=jnp.float32,
            )
            * scale
        )
        allowed = (query_doc[:, None] == doc_block[None, :]) & (
            pos_block[None, :] <= query_pos[:, None]
        )
        scores = jnp.where(allowed, scores, NEGATIVE)
        updated = jnp.maximum(largest, jnp.max(scores, axis=-1))
        weights = jnp.where(allowed, jnp.exp(scores - updated[..., None]), 0.0)
        factor = jnp.exp(largest - updated)
        totals = totals * factor + jnp.sum(weights, axis=-1)
        mixed = jnp.einsum(
            "gpqk,kgd->gpqd",
            weights.astype(jnp.bfloat16),
            value_block.reshape(block, groups, head_size),
            preferred_element_type=jnp.float32,
        )
        return (updated, totals, accum * factor[..., None] + mixed)

    def visit(current, item):
        key_block, value_block, pos_block, doc_block = item
        result = lax.cond(
            pos_block[0] <= newest,
            lambda inner: compute(inner, key_block, value_block, pos_block, doc_block),
            lambda inner: inner,
            current,
        )
        return (result, None)

    items = (
        keys_piece.reshape(blocks, block, -1),
        values_piece.reshape(blocks, block, -1),
        key_pos.reshape(blocks, block),
        key_doc.reshape(blocks, block),
    )
    final, unused = lax.scan(visit, state, items)
    return final


def finish(totals, accum):
    queried = accum.shape[2]
    result = accum / totals[..., None]
    return jnp.transpose(result, (2, 0, 1, 3)).reshape(queried, -1).astype(jnp.bfloat16)


def gathered(teacher_q, teacher_k, teacher_v, student_q, student_k, student_v, doc_ids, proj_weight):
    shard_rows = teacher_q.shape[0]
    groups = teacher_k.shape[1] // TD
    outer = lax.axis_size("pb")
    inner_size = lax.axis_size("kv")
    total_tokens = shard_rows * outer * inner_size
    shard = lax.axis_index("pb") * inner_size + lax.axis_index("kv")
    own_pos = shard * shard_rows + jnp.arange(shard_rows, dtype=jnp.int32)
    initial = (start_state(teacher_q, TD, groups), start_state(student_q, SD, groups))
    key_teacher = lax.all_gather(teacher_k, ("pb", "kv"), axis=0, tiled=True)
    value_teacher = lax.all_gather(teacher_v, ("pb", "kv"), axis=0, tiled=True)
    key_student = lax.all_gather(student_k, ("pb", "kv"), axis=0, tiled=True)
    value_student = lax.all_gather(student_v, ("pb", "kv"), axis=0, tiled=True)
    piece_doc = lax.all_gather(doc_ids, ("pb", "kv"), axis=0, tiled=True)
    key_pos = jnp.arange(piece_doc.shape[0], dtype=jnp.int32)
    teacher_state = attend_keys(
        initial[0], teacher_q, own_pos, doc_ids, key_teacher, value_teacher, key_pos, piece_doc, TD
    )
    student_state = attend_keys(
        initial[1], student_q, own_pos, doc_ids, key_student, value_student, key_pos, piece_doc, SD
    )
    teacher_state, student_state = (teacher_state, student_state)
    teacher_out = finish(teacher_state[1], teacher_state[2])
    student_out = finish(student_state[1], student_state[2])
    teacher_half, student_half = (
        lax.all_to_all(teacher_out, "ha", split_axis=0, concat_axis=1, tiled=True),
        lax.all_to_all(student_out, "ha", split_axis=0, concat_axis=1, tiled=True),
    )
    count = teacher_half.shape[0]
    heads = proj_weight.shape[0]
    teacher_float = teacher_half.astype(jnp.float32)
    target = teacher_float * lax.rsqrt(
        jnp.mean(teacher_float * teacher_float, axis=1, keepdims=True) + EPSILON
    )
    student_float = student_half.astype(jnp.float32)
    features = (
        student_float
        * lax.rsqrt(jnp.mean(student_float * student_float, axis=1, keepdims=True) + EPSILON)
    ).astype(jnp.bfloat16)
    feature_heads = features.reshape(count, heads, -1)
    predicted = jnp.einsum(
        "thd,hde->the", feature_heads, proj_weight, preferred_element_type=jnp.float32
    )
    difference = predicted.reshape(count, -1) - target
    token_loss = jnp.mean(difference * difference, axis=1)
    gradient = jnp.einsum(
        "thd,the->hde",
        feature_heads.astype(jnp.float32),
        difference.reshape(count, heads, -1),
        precision=lax.Precision.HIGHEST,
    )
    gradient = (gradient / math.sqrt(total_tokens)).reshape(-1, gradient.shape[2])
    grad_w = lax.psum_scatter(gradient, ("pb", "kv", "ha"), scatter_dimension=0, tiled=True)
    return (grad_w, token_loss)

def rows_dot(a, b):
    return lax.dot_general(a, b, (((1,), (1,)), ((), ())), preferred_element_type=jnp.float32)


def columns_dot(a, b):
    return lax.dot_general(a, b, (((0,), (0,)), ((), ())), preferred_element_type=jnp.float32)


def fused(
    shape,
    tokens,
    tq_ref,
    tk_hbm,
    tv_hbm,
    sq_ref,
    sk_hbm,
    sv_hbm,
    doc_hbm,
    w_hbm,
    grad_ref,
    loss_ref,
    tk_ref,
    tv_ref,
    sk_ref,
    sv_ref,
    doc_ref,
    w_ref,
    stage,
    kv,
    tq_in,
    sq_in,
    tq_all,
    sq_all,
    t_acc,
    s_acc,
    soft,
    stats,
    losses,
    grads,
    grads_in,
    xy_send,
    xy_recv,
    q_send,
    q_recv,
    up_send,
    up_recv,
    down_send,
    down_recv,
    stat_send,
    stat_recv,
    loss_send,
    loss_recv,
    grad_send,
    grad_recv,
    load_sem,
):
    npb, nkv, nha = shape
    devices = npb * nkv * nha
    rows = tq_ref.shape[0]
    heads = tq_ref.shape[1] // (npb * TD)
    wide = heads * rows
    pb, z, ha = lax.axis_index("pb"), lax.axis_index("kv"), lax.axis_index("ha")
    me = (pb * nkv + z) * nha + ha

    def coords(index):
        return (index // (nkv * nha), (index // nha) % nkv, index % nha)

    first_head = (ha * npb + pb) * heads

    def query_part(place, which):
        ref, width = ((tq_ref, heads * TD), (sq_ref, heads * SD))[which]
        return ref.at[:, pl.ds(pl.multiple_of(place * width, width), width)]

    loads = [
        pltpu.make_async_copy(source, into, load_sem.at[i])
        for i, (source, into) in enumerate(
            (
                (tk_hbm, tk_ref),
                (tv_hbm, tv_ref),
                (sk_hbm, sk_ref),
                (sv_hbm, sv_ref),
                (doc_hbm, doc_ref),
                (w_hbm.at[pl.ds(first_head, heads)], w_ref),
                (query_part(pb, 0), tq_in.at[pb]),
                (query_part(pb, 1), sq_in.at[pb]),
            )
        )
    ]
    for load in loads:
        load.start()

    barrier = pltpu.get_barrier_semaphore()

    def greet(r, carry):
        pl.semaphore_signal(
            barrier, inc=1, device_id=coords((me + r) % devices), device_id_type=MESH
        )
        return carry

    lax.fori_loop(1, devices, greet, 0)

    for load in loads[:5]:
        load.wait()
    doc_rows = jnp.broadcast_to(doc_ref[...].astype(jnp.float32), (16, rows)).astype(jnp.bfloat16)
    for g in range(npb):
        stage[g, 0:rows, :] = tk_ref[:, g * TD : (g + 1) * TD]
        stage[g, rows : 2 * rows, :] = (
            tv_ref[:, g * TD : (g + 1) * TD].astype(jnp.float32).T.astype(jnp.bfloat16)
        )
        stage[g, 2 * rows : 3 * rows, :] = jnp.concatenate(
            [sk_ref[:, g * SD : (g + 1) * SD], sv_ref[:, g * SD : (g + 1) * SD]], axis=1
        )
        stage[g, 3 * rows : 3 * rows + 16, :] = doc_rows
    kv[z, pb] = stage[pb]

    pl.semaphore_wait(barrier, devices - 1)

    def partner(r):
        return ((pb // 2 + r // 2) % 2) * 2 + (pb % 2 + r % 2) % 2

    def kv_copy(r):
        to = partner(r)
        return pltpu.make_async_remote_copy(
            src_ref=stage.at[to],
            dst_ref=kv.at[z, pb],
            send_sem=xy_send.at[r],
            recv_sem=xy_recv.at[r],
            device_id=(to, z, ha),
            device_id_type=MESH,
        )

    def q_copy(r, which):
        to = partner(r)
        return pltpu.make_async_remote_copy(
            src_ref=query_part(to, which),
            dst_ref=(tq_in, sq_in)[which].at[pb],
            send_sem=q_send.at[r, which],
            recv_sem=q_recv.at[r, which],
            device_id=(to, z, ha),
            device_id_type=MESH,
        )

    for r in range(1, npb):
        kv_copy(r).start()

    def chain(h, c, up):
        piece = kv.at[z - h if up else z + h, c]
        send, recv = (up_send, up_recv) if up else (down_send, down_recv)
        return pltpu.make_async_remote_copy(
            src_ref=piece,
            dst_ref=piece,
            send_sem=send.at[h, c],
            recv_sem=recv.at[h, c],
            device_id=(pb, z + 1 if up else z - 1, ha),
            device_id_type=MESH,
        )

    def arrived(h, c, up):
        piece = kv.at[z - h if up else z + h, c]
        send, recv = (up_send, up_recv) if up else (down_send, down_recv)
        pltpu.make_async_remote_copy(
            src_ref=piece,
            dst_ref=piece,
            send_sem=send.at[h - 1, c],
            recv_sem=recv.at[h - 1, c],
            device_id=(pb, z - 1 if up else z + 1, ha),
            device_id_type=MESH,
        ).wait_recv()

    for r in range(npb):
        if r > 0:
            kv_copy(r).wait_recv()

        @pl.when(z < nkv - 1)
        def _():
            chain(0, partner(r), True).start()

        @pl.when((z > 0) & (partner(r) < npb - 1))
        def _():
            chain(0, partner(r), False).start()

    for r in range(1, npb):
        q_copy(r, 0).start()
        q_copy(r, 1).start()

    def next_hop(h, c):
        @pl.when(z - h >= 0)
        def _():
            arrived(h, c, True)

            @pl.when(z < nkv - 1)
            def _():
                chain(h, c, True).start()

        if not isinstance(c, int) or c < npb - 1:

            @pl.when((z + h <= nkv - 1) & (c < npb - 1))
            def _():
                arrived(h, c, False)

                @pl.when(z > 0)
                def _():
                    chain(h, c, False).start()

    t_acc[...] = jnp.zeros_like(t_acc)
    s_acc[...] = jnp.zeros_like(s_acc)
    soft[:, 0:2, :] = jnp.full((npb, 2, wide), NEGATIVE, jnp.float32)
    soft[:, 2:4, :] = jnp.zeros((npb, 2, wide), jnp.float32)

    local_key = lax.broadcasted_iota(jnp.int32, (rows, wide), 0)
    local_query = lax.broadcasted_iota(jnp.int32, (1, wide), 1) % rows
    float_key = local_key.astype(jnp.float32)
    float_query = local_query.astype(jnp.float32)

    def masked_scores(source, p, first, last, own_place):
        own = kv[z, p, 3 * rows : 3 * rows + 16, :].astype(jnp.float32)[0:1, :]
        query_doc = jnp.concatenate([own] * heads, axis=1)
        firsts = []
        for c in range(first, last):
            key_doc = kv[source, c, 3 * rows : 3 * rows + 16, :].astype(jnp.float32)[0:1, :]
            least = jnp.zeros((1, wide), jnp.float32)
            for d in range(1, DOCS):
                before = jnp.sum((key_doc < d).astype(jnp.float32), axis=1, keepdims=True)
                least = jnp.where(query_doc == d, before, least)
            firsts.append(least)

        def allowed(c, which):
            if which == 0:
                ok = local_key >= firsts[c - first].astype(jnp.int32)
                return ok & (local_key <= local_query) if own_place and c == p else ok
            ok = float_key > firsts[c - first] - 0.5
            return ok & (float_key < float_query + 0.5) if own_place and c == p else ok

        result = []
        for which in range(2):
            cut = slice(0, rows) if which == 0 else slice(2 * rows, 3 * rows)
            key_rows = kv[source, first:last, cut, :].reshape((last - first) * rows, TD)
            raw = rows_dot(key_rows, (tq_all, sq_all)[which][p])
            result.append(
                jnp.concatenate(
                    [
                        jnp.where(
                            allowed(c, which),
                            raw[(c - first) * rows : (c - first + 1) * rows],
                            NEGATIVE,
                        )
                        for c in range(first, last)
                    ],
                    axis=0,
                )
            )
        return result

    def absorb(source, p, first, last, which, scores):
        factor = 1.0 / math.sqrt(TD) if which == 0 else 1.0
        old = soft[p, which : which + 1, :]
        new = jnp.maximum(old, jnp.max(scores, axis=0, keepdims=True))
        weights = jnp.exp((scores - new) * factor)
        shrink = jnp.exp((old - new) * factor)
        soft[p, which : which + 1, :] = new
        soft[p, which + 2 : which + 3, :] = soft[
            p, which + 2 : which + 3, :
        ] * shrink + jnp.sum(weights, axis=0, keepdims=True)
        rounded = weights.astype(jnp.bfloat16)
        if which == 0:
            values = jnp.concatenate(
                [kv[source, c, rows : 2 * rows, :] for c in range(first, last)], axis=1
            )
            t_acc[p] = t_acc[p] * shrink + jnp.dot(
                values, rounded, preferred_element_type=jnp.float32
            )
        else:
            key_rows = kv[source, first:last, 2 * rows : 3 * rows, :]
            key_rows = key_rows.reshape((last - first) * rows, TD)
            s_acc[p] = s_acc[p] * shrink + columns_dot(key_rows, rounded)[TD - SD :]

    def attend(source, blocks, own_place=False):
        scores = masked_scores(source, *blocks[0], own_place)
        for i, block in enumerate(blocks):
            later = None
            if i + 1 < len(blocks):
                later = masked_scores(source, *blocks[i + 1], own_place)
            for which in range(2):
                absorb(source, *block, which, scores[which])
            scores = later

    for load in loads[5:]:
        load.wait()
    blank = jnp.zeros((rows, TD - SD), jnp.bfloat16)
    scale = jnp.asarray(1.0 / math.sqrt(SD), jnp.bfloat16)

    def own_turn(r, carry):
        place = partner(r)

        @pl.when(r > 0)
        def _():
            q_copy(r, 0).wait_recv()
            q_copy(r, 1).wait_recv()

        for j in range(heads):
            tq_all[place, j * rows : (j + 1) * rows, :] = tq_in[place, :, j * TD : (j + 1) * TD]
            sq_all[place, j * rows : (j + 1) * rows, :] = jnp.concatenate(
                [sq_in[place, :, j * SD : (j + 1) * SD] * scale, blank], axis=1
            )
        for p in range(npb):

            @pl.when(place == p)
            def _():
                attend(z, [(p, 0, p + 1)], True)

        next_hop(1, place)
        return carry

    lax.fori_loop(0, npb, own_turn, 0)

    def hops(h, early, pieces):
        for c in pieces:

            @pl.when(((h >= 2) & (h <= nkv - 2)) if early else (h == nkv - 1))
            def _():
                next_hop(h, c)

    def turn(h, carry):
        hops(h + 1, True, range(1))
        hops(h, False, range(npb - 1))

        @pl.when(z - h >= 0)
        def _():
            attend(z - h, [(p, 0, min(p + 1, npb - 1)) for p in range(npb)])

        hops(h + 1, True, range(1, npb - 1))
        hops(h, False, range(npb - 1, npb))

        @pl.when(z - h >= 0)
        def _():
            attend(z - h, [(npb - 1, npb - 1, npb)])

        hops(h + 1, True, range(npb - 1, npb))

        @pl.when(z + h <= nkv - 1)
        def _():
            attend(z + h, [(p, 0, p) for p in range(1, npb)])

        return carry

    lax.fori_loop(1, nkv, turn, 0)

    def by_token(row):
        total = row[:, 0:rows]
        for j in range(1, heads):
            total = total + row[:, j * rows : (j + 1) * rows]
        return total

    t_sums, s_sums, t_outs, s_outs = [], [], [], []
    for p in range(npb):
        t_out = (t_acc[p] / soft[p, 2:3, :]).astype(jnp.bfloat16).astype(jnp.float32)
        s_out = (s_acc[p] / soft[p, 3:4, :]).astype(jnp.bfloat16).astype(jnp.float32)
        t_acc[p] = t_out
        s_acc[p] = s_out
        t_sums.append(by_token(jnp.sum(t_out * t_out, axis=0, keepdims=True)))
        s_sums.append(by_token(jnp.sum(s_out * s_out, axis=0, keepdims=True)))

    plane = npb * nha
    slot = pb * nha + ha

    def share(buffer, send, recv, r):
        to = (slot + r) % plane
        return pltpu.make_async_remote_copy(
            src_ref=buffer.at[slot],
            dst_ref=buffer.at[slot],
            send_sem=send.at[r],
            recv_sem=recv.at[r],
            device_id=(to // nha, z, to % nha),
            device_id_type=MESH,
        )

    stats[slot] = jnp.concatenate(t_sums + s_sums, axis=0)
    for r in range(1, plane):
        share(stats, stat_send, stat_recv, r).start()
    for r in range(1, plane):
        share(stats, stat_send, stat_recv, r).wait_recv()
    sums = stats[0]
    for i in range(1, plane):
        sums = sums + stats[i]
    t_scale = lax.rsqrt(sums[0:npb] * (1.0 / (heads * plane * TD)) + EPSILON)
    s_scale = lax.rsqrt(sums[npb : 2 * npb] * (1.0 / (heads * plane * SD)) + EPSILON)

    def grad_copy(j):
        return pltpu.make_async_remote_copy(
            src_ref=grads.at[j],
            dst_ref=grads_in.at[z],
            send_sem=grad_send.at[j],
            recv_sem=grad_recv.at[z],
            device_id=coords(first_head + j),
            device_id_type=MESH,
        )

    loss = jnp.zeros((1, npb * rows), jnp.float32)
    for j in range(heads):
        cut = slice(j * rows, (j + 1) * rows)
        target = jnp.concatenate(
            [t_acc[p, :, cut] * t_scale[p : p + 1] for p in range(npb)], axis=1
        )
        feature = jnp.concatenate(
            [s_acc[p, :, cut] * s_scale[p : p + 1] for p in range(npb)], axis=1
        ).astype(jnp.bfloat16)
        difference = columns_dot(w_ref[j], feature) - target
        high = difference.astype(jnp.bfloat16)
        low = (difference - high.astype(jnp.float32)).astype(jnp.bfloat16)
        grads[j] = rows_dot(feature, high) + rows_dot(feature, low)

        @pl.when(first_head + j != me)
        def _():
            grad_copy(j).start()

        @pl.when(first_head + j == me)
        def _():
            grads_in[z] = grads[j]

        loss = loss + jnp.sum(difference * difference, axis=0, keepdims=True)
    losses[slot] = jnp.concatenate(
        [loss[:, p * rows : (p + 1) * rows] for p in range(npb)]
        + [jnp.zeros((8 - npb, rows), jnp.float32)],
        axis=0,
    )
    for r in range(1, plane):
        share(losses, loss_send, loss_recv, r).start()

    for r in range(1, plane):
        share(losses, loss_send, loss_recv, r).wait_recv()
    mine = losses[0, pl.ds(pb, 1), :]
    for i in range(1, plane):
        mine = mine + losses[i, pl.ds(pb, 1), :]
    part = rows // nha
    chosen = mine[:, 0:part]
    for i in range(1, nha):
        chosen = jnp.where(ha == i, mine[:, i * part : (i + 1) * part], chosen)
    loss_ref[...] = chosen * (1.0 / (heads * plane * TD))

    giver_ha = me // (npb * heads)
    giver_pb = (me // heads) % npb
    for i in range(nkv):

        @pl.when((giver_ha != ha) | (giver_pb != pb) | (z != i))
        def _():
            pltpu.make_async_remote_copy(
                src_ref=grads.at[0],
                dst_ref=grads_in.at[i],
                send_sem=grad_send.at[0],
                recv_sem=grad_recv.at[i],
                device_id=(giver_pb, i, giver_ha),
                device_id_type=MESH,
            ).wait_recv()

    total = grads_in[0]
    for i in range(1, nkv):
        total = total + grads_in[i]
    grad_ref[...] = total * (1.0 / math.sqrt(tokens))

    for r in range(1, npb):
        kv_copy(r).wait_send()
        q_copy(r, 0).wait_send()
        q_copy(r, 1).wait_send()
    for h in range(nkv - 1):
        for c in range(npb):

            @pl.when((z - h >= 0) & (z < nkv - 1))
            def _():
                chain(h, c, True).wait_send()

            if c < npb - 1:

                @pl.when((z + h <= nkv - 1) & (z > 0))
                def _():
                    chain(h, c, False).wait_send()

    for r in range(1, plane):
        share(stats, stat_send, stat_recv, r).wait_send()
        share(losses, loss_send, loss_recv, r).wait_send()
    for j in range(heads):

        @pl.when(first_head + j != me)
        def _():
            grad_copy(j).wait_send()


def by_heads(
    shape, teacher_q, teacher_k, teacher_v, student_q, student_k, student_v, doc_ids, proj_weight
):
    npb, nkv, nha = shape
    rows = teacher_q.shape[0]
    heads = teacher_q.shape[1] // (npb * TD)
    wide = heads * rows
    plane = npb * nha
    dma = pltpu.SemaphoreType.DMA
    bf16, f32 = jnp.bfloat16, jnp.float32
    vmem = pl.BlockSpec(memory_space=pltpu.VMEM)
    grad, loss = pl.pallas_call(
        functools.partial(fused, shape, rows * npb * nkv),
        out_shape=(
            jax.ShapeDtypeStruct((SD, TD), f32),
            jax.ShapeDtypeStruct((1, rows // nha), f32),
        ),
        in_specs=[pl.BlockSpec(memory_space=pltpu.HBM)] * 8,
        out_specs=(vmem, vmem),
        scratch_shapes=[
            pltpu.VMEM(teacher_k.shape, bf16),
            pltpu.VMEM(teacher_v.shape, bf16),
            pltpu.VMEM(student_k.shape, bf16),
            pltpu.VMEM(student_v.shape, bf16),
            pltpu.VMEM((1, rows), jnp.int32),
            pltpu.VMEM((heads, SD, TD), bf16),
            pltpu.VMEM((npb, 3 * rows + 16, TD), bf16),
            pltpu.VMEM((nkv, npb, 3 * rows + 16, TD), bf16),
            pltpu.VMEM((npb, rows, heads * TD), bf16),
            pltpu.VMEM((npb, rows, heads * SD), bf16),
            pltpu.VMEM((npb, wide, TD), bf16),
            pltpu.VMEM((npb, wide, TD), bf16),
            pltpu.VMEM((npb, TD, wide), f32),
            pltpu.VMEM((npb, SD, wide), f32),
            pltpu.VMEM((npb, 8, wide), f32),
            pltpu.VMEM((plane, 8, rows), f32),
            pltpu.VMEM((plane, 8, rows), f32),
            pltpu.VMEM((heads, SD, TD), f32),
            pltpu.VMEM((nkv, SD, TD), f32),
            dma((npb,)),
            dma((npb,)),
            dma((npb, 2)),
            dma((npb, 2)),
            dma((nkv, npb)),
            dma((nkv, npb)),
            dma((nkv, npb)),
            dma((nkv, npb)),
            dma((plane,)),
            dma((plane,)),
            dma((plane,)),
            dma((plane,)),
            dma((heads,)),
            dma((nkv,)),
            dma((8,)),
        ],
        compiler_params=pltpu.CompilerParams(
            collective_id=0, has_side_effects=True, vmem_limit_bytes=63 * 1024 * 1024
        ),
        name="attention_distillation",
    )(
        teacher_q,
        teacher_k,
        teacher_v,
        student_q,
        student_k,
        student_v,
        doc_ids.reshape(1, rows),
        proj_weight,
    )
    return grad, loss.reshape(-1)


def local(*arguments):
    teacher_q, teacher_k, proj_weight = arguments[0], arguments[1], arguments[7]
    shape = tuple(lax.axis_size(name) for name in ("pb", "kv", "ha"))
    groups = teacher_k.shape[1] // TD
    fits = (
        groups == shape[0] == 4
        and shape[2] == 2
        and math.prod(shape) == proj_weight.shape[0]
        and teacher_q.shape[0] == 128
    )
    if fits:
        return by_heads(shape, *arguments)
    return gathered(*arguments)


def solution(mesh):
    in_specs = (
        P(("pb", "kv"), "ha"),
        P(("pb", "kv"), "ha"),
        P(("pb", "kv"), "ha"),
        P(("pb", "kv"), "ha"),
        P(("pb", "kv"), "ha"),
        P(("pb", "kv"), "ha"),
        P(("pb", "kv")),
        P(),
    )
    out_specs = (P(("pb", "kv", "ha"), None), P(("pb", "kv", "ha")))
    return jax.shard_map(local, mesh=mesh, in_specs=in_specs, out_specs=out_specs, check_vma=False)
```

```python
import functools
import math

import jax
import jax.numpy as jnp
from jax import lax
from jax.experimental import pallas as pl
from jax.experimental.pallas import tpu as pltpu
from jax.sharding import PartitionSpec as P

MESH = pl.DeviceIdType.MESH

TD = 128
SD = 64
DOCS = 4


NEGATIVE = -1e30
EPSILON = 1e-06


def start_state(queries, head_size, groups):
    queried = queries.shape[0]
    per_group = queries.shape[1] // (groups * head_size)
    largest = jnp.full((groups, per_group, queried), NEGATIVE, jnp.float32)
    totals = jnp.zeros((groups, per_group, queried), jnp.float32)
    accum = jnp.zeros((groups, per_group, queried, head_size), jnp.float32)
    return (largest, totals, accum)


def attend_keys(
    state, queries, query_pos, query_doc, keys_piece, values_piece, key_pos, key_doc, head_size
):
    length = keys_piece.shape[0]
    block = math.gcd(length, 512)
    blocks = length // block
    groups = keys_piece.shape[1] // head_size
    queried = queries.shape[0]
    per_group = queries.shape[1] // (groups * head_size)
    shaped = queries.reshape(queried, groups, per_group, head_size)
    scale = 1.0 / math.sqrt(head_size)
    newest = jnp.max(query_pos)

    def compute(current, key_block, value_block, pos_block, doc_block):
        largest, totals, accum = current
        scores = (
            jnp.einsum(
                "qgpd,kgd->gpqk",
                shaped,
                key_block.reshape(block, groups, head_size),
                preferred_element_type=jnp.float32,
            )
            * scale
        )
        allowed = (query_doc[:, None] == doc_block[None, :]) & (
            pos_block[None, :] <= query_pos[:, None]
        )
        scores = jnp.where(allowed, scores, NEGATIVE)
        updated = jnp.maximum(largest, jnp.max(scores, axis=-1))
        weights = jnp.where(allowed, jnp.exp(scores - updated[..., None]), 0.0)
        factor = jnp.exp(largest - updated)
        totals = totals * factor + jnp.sum(weights, axis=-1)
        mixed = jnp.einsum(
            "gpqk,kgd->gpqd",
            weights.astype(jnp.bfloat16),
            value_block.reshape(block, groups, head_size),
            preferred_element_type=jnp.float32,
        )
        return (updated, totals, accum * factor[..., None] + mixed)

    def visit(current, item):
        key_block, value_block, pos_block, doc_block = item
        result = lax.cond(
            pos_block[0] <= newest,
            lambda inner: compute(inner, key_block, value_block, pos_block, doc_block),
            lambda inner: inner,
            current,
        )
        return (result, None)

    items = (
        keys_piece.reshape(blocks, block, -1),
        values_piece.reshape(blocks, block, -1),
        key_pos.reshape(blocks, block),
        key_doc.reshape(blocks, block),
    )
    final, unused = lax.scan(visit, state, items)
    return final


def finish(totals, accum):
    queried = accum.shape[2]
    result = accum / totals[..., None]
    return jnp.transpose(result, (2, 0, 1, 3)).reshape(queried, -1).astype(jnp.bfloat16)


def gathered(teacher_q, teacher_k, teacher_v, student_q, student_k, student_v, doc_ids, proj_weight):
    shard_rows = teacher_q.shape[0]
    groups = teacher_k.shape[1] // TD
    outer = lax.axis_size("pb")
    inner_size = lax.axis_size("kv")
    total_tokens = shard_rows * outer * inner_size
    shard = lax.axis_index("pb") * inner_size + lax.axis_index("kv")
    own_pos = shard * shard_rows + jnp.arange(shard_rows, dtype=jnp.int32)
    initial = (start_state(teacher_q, TD, groups), start_state(student_q, SD, groups))
    key_teacher = lax.all_gather(teacher_k, ("pb", "kv"), axis=0, tiled=True)
    value_teacher = lax.all_gather(teacher_v, ("pb", "kv"), axis=0, tiled=True)
    key_student = lax.all_gather(student_k, ("pb", "kv"), axis=0, tiled=True)
    value_student = lax.all_gather(student_v, ("pb", "kv"), axis=0, tiled=True)
    piece_doc = lax.all_gather(doc_ids, ("pb", "kv"), axis=0, tiled=True)
    key_pos = jnp.arange(piece_doc.shape[0], dtype=jnp.int32)
    teacher_state = attend_keys(
        initial[0], teacher_q, own_pos, doc_ids, key_teacher, value_teacher, key_pos, piece_doc, TD
    )
    student_state = attend_keys(
        initial[1], student_q, own_pos, doc_ids, key_student, value_student, key_pos, piece_doc, SD
    )
    teacher_state, student_state = (teacher_state, student_state)
    teacher_out = finish(teacher_state[1], teacher_state[2])
    student_out = finish(student_state[1], student_state[2])
    teacher_half, student_half = (
        lax.all_to_all(teacher_out, "ha", split_axis=0, concat_axis=1, tiled=True),
        lax.all_to_all(student_out, "ha", split_axis=0, concat_axis=1, tiled=True),
    )
    count = teacher_half.shape[0]
    heads = proj_weight.shape[0]
    teacher_float = teacher_half.astype(jnp.float32)
    target = teacher_float * lax.rsqrt(
        jnp.mean(teacher_float * teacher_float, axis=1, keepdims=True) + EPSILON
    )
    student_float = student_half.astype(jnp.float32)
    features = (
        student_float
        * lax.rsqrt(jnp.mean(student_float * student_float, axis=1, keepdims=True) + EPSILON)
    ).astype(jnp.bfloat16)
    feature_heads = features.reshape(count, heads, -1)
    predicted = jnp.einsum(
        "thd,hde->the", feature_heads, proj_weight, preferred_element_type=jnp.float32
    )
    difference = predicted.reshape(count, -1) - target
    token_loss = jnp.mean(difference * difference, axis=1)
    gradient = jnp.einsum(
        "thd,the->hde",
        feature_heads.astype(jnp.float32),
        difference.reshape(count, heads, -1),
        precision=lax.Precision.HIGHEST,
    )
    gradient = (gradient / math.sqrt(total_tokens)).reshape(-1, gradient.shape[2])
    grad_w = lax.psum_scatter(gradient, ("pb", "kv", "ha"), scatter_dimension=0, tiled=True)
    return (grad_w, token_loss)

def rows_dot(a, b):
    return lax.dot_general(a, b, (((1,), (1,)), ((), ())), preferred_element_type=jnp.float32)


def columns_dot(a, b):
    return lax.dot_general(a, b, (((0,), (0,)), ((), ())), preferred_element_type=jnp.float32)


def fused(
    shape,
    tokens,
    tq_ref,
    tk_hbm,
    tv_hbm,
    sq_ref,
    sk_hbm,
    sv_hbm,
    doc_hbm,
    w_hbm,
    grad_ref,
    loss_ref,
    tk_ref,
    tv_ref,
    sk_ref,
    sv_ref,
    doc_ref,
    w_ref,
    stage,
    kv,
    tq_in,
    sq_in,
    tq_all,
    sq_all,
    t_acc,
    s_acc,
    soft,
    stats,
    losses,
    grads,
    grads_in,
    xy_send,
    xy_recv,
    q_send,
    q_recv,
    up_send,
    up_recv,
    down_send,
    down_recv,
    stat_send,
    stat_recv,
    loss_send,
    loss_recv,
    grad_send,
    grad_recv,
    load_sem,
):
    npb, nkv, nha = shape
    devices = npb * nkv * nha
    rows = tq_ref.shape[0]
    heads = tq_ref.shape[1] // (npb * TD)
    wide = heads * rows
    pb, z, ha = lax.axis_index("pb"), lax.axis_index("kv"), lax.axis_index("ha")
    me = (pb * nkv + z) * nha + ha

    def coords(index):
        return (index // (nkv * nha), (index // nha) % nkv, index % nha)

    first_head = (ha * npb + pb) * heads

    def query_part(place, which):
        ref, width = ((tq_ref, heads * TD), (sq_ref, heads * SD))[which]
        return ref.at[:, pl.ds(pl.multiple_of(place * width, width), width)]

    loads = [
        pltpu.make_async_copy(source, into, load_sem.at[i])
        for i, (source, into) in enumerate(
            (
                (tk_hbm, tk_ref),
                (tv_hbm, tv_ref),
                (sk_hbm, sk_ref),
                (sv_hbm, sv_ref),
                (doc_hbm, doc_ref),
                (w_hbm.at[pl.ds(first_head, heads)], w_ref),
                (query_part(pb, 0), tq_in.at[pb]),
                (query_part(pb, 1), sq_in.at[pb]),
            )
        )
    ]
    for load in loads:
        load.start()

    barrier = pltpu.get_barrier_semaphore()

    def greet(r, carry):
        pl.semaphore_signal(
            barrier, inc=1, device_id=coords((me + r) % devices), device_id_type=MESH
        )
        return carry

    lax.fori_loop(1, devices, greet, 0)

    for load in loads[:5]:
        load.wait()
    doc_rows = jnp.broadcast_to(doc_ref[...].astype(jnp.float32), (16, rows)).astype(jnp.bfloat16)
    for g in range(npb):
        stage[g, 0:rows, :] = tk_ref[:, g * TD : (g + 1) * TD]
        stage[g, rows : 2 * rows, :] = (
            tv_ref[:, g * TD : (g + 1) * TD].astype(jnp.float32).T.astype(jnp.bfloat16)
        )
        stage[g, 2 * rows : 3 * rows, :] = jnp.concatenate(
            [sk_ref[:, g * SD : (g + 1) * SD], sv_ref[:, g * SD : (g + 1) * SD]], axis=1
        )
        stage[g, 3 * rows : 3 * rows + 16, :] = doc_rows
    kv[z, pb] = stage[pb]

    pl.semaphore_wait(barrier, devices - 1)

    def partner(r):
        return ((pb // 2 + r // 2) % 2) * 2 + (pb % 2 + r % 2) % 2

    def kv_copy(r):
        to = partner(r)
        return pltpu.make_async_remote_copy(
            src_ref=stage.at[to],
            dst_ref=kv.at[z, pb],
            send_sem=xy_send.at[r],
            recv_sem=xy_recv.at[r],
            device_id=(to, z, ha),
            device_id_type=MESH,
        )

    def q_copy(r, which):
        to = partner(r)
        return pltpu.make_async_remote_copy(
            src_ref=query_part(to, which),
            dst_ref=(tq_in, sq_in)[which].at[pb],
            send_sem=q_send.at[r, which],
            recv_sem=q_recv.at[r, which],
            device_id=(to, z, ha),
            device_id_type=MESH,
        )

    for r in range(1, npb):
        kv_copy(r).start()
    for r in range(1, npb):
        q_copy(r, 0).start()
        q_copy(r, 1).start()

    def chain(h, c, up):
        piece = kv.at[z - h if up else z + h, c]
        send, recv = (up_send, up_recv) if up else (down_send, down_recv)
        return pltpu.make_async_remote_copy(
            src_ref=piece,
            dst_ref=piece,
            send_sem=send.at[h, c],
            recv_sem=recv.at[h, c],
            device_id=(pb, z + 1 if up else z - 1, ha),
            device_id_type=MESH,
        )

    def arrived(h, c, up):
        piece = kv.at[z - h if up else z + h, c]
        send, recv = (up_send, up_recv) if up else (down_send, down_recv)
        pltpu.make_async_remote_copy(
            src_ref=piece,
            dst_ref=piece,
            send_sem=send.at[h - 1, c],
            recv_sem=recv.at[h - 1, c],
            device_id=(pb, z - 1 if up else z + 1, ha),
            device_id_type=MESH,
        ).wait_recv()

    for r in range(npb):
        if r > 0:
            kv_copy(r).wait_recv()

        @pl.when(z < nkv - 1)
        def _():
            chain(0, partner(r), True).start()

        @pl.when((z > 0) & (partner(r) < npb - 1))
        def _():
            chain(0, partner(r), False).start()

    def next_hop(h, c):
        @pl.when(z - h >= 0)
        def _():
            arrived(h, c, True)

            @pl.when(z < nkv - 1)
            def _():
                chain(h, c, True).start()

        if not isinstance(c, int) or c < npb - 1:

            @pl.when((z + h <= nkv - 1) & (c < npb - 1))
            def _():
                arrived(h, c, False)

                @pl.when(z > 0)
                def _():
                    chain(h, c, False).start()

    t_acc[...] = jnp.zeros_like(t_acc)
    s_acc[...] = jnp.zeros_like(s_acc)
    soft[:, 0:2, :] = jnp.full((npb, 2, wide), NEGATIVE, jnp.float32)
    soft[:, 2:4, :] = jnp.zeros((npb, 2, wide), jnp.float32)

    local_key = lax.broadcasted_iota(jnp.int32, (rows, wide), 0)
    local_query = lax.broadcasted_iota(jnp.int32, (1, wide), 1) % rows
    float_key = local_key.astype(jnp.float32)
    float_query = local_query.astype(jnp.float32)

    def masked_scores(source, p, count, own_place):
        own = kv[z, p, 3 * rows : 3 * rows + 16, :].astype(jnp.float32)[0:1, :]
        query_doc = jnp.concatenate([own] * heads, axis=1)
        firsts = []
        for c in range(count):
            key_doc = kv[source, c, 3 * rows : 3 * rows + 16, :].astype(jnp.float32)[0:1, :]
            least = jnp.zeros((1, wide), jnp.float32)
            for d in range(1, DOCS):
                before = jnp.sum((key_doc < d).astype(jnp.float32), axis=1, keepdims=True)
                least = jnp.where(query_doc == d, before, least)
            firsts.append(least)

        def allowed(c, which):
            if which == 0:
                ok = local_key >= firsts[c].astype(jnp.int32)
                return ok & (local_key <= local_query) if own_place and c == p else ok
            ok = float_key > firsts[c] - 0.5
            return ok & (float_key < float_query + 0.5) if own_place and c == p else ok

        result = []
        for which in range(2):
            cut = slice(0, rows) if which == 0 else slice(2 * rows, 3 * rows)
            key_rows = kv[source, 0:count, cut, :].reshape(count * rows, TD)
            raw = rows_dot(key_rows, (tq_all, sq_all)[which][p])
            result.append(
                jnp.concatenate(
                    [
                        jnp.where(allowed(c, which), raw[c * rows : (c + 1) * rows], NEGATIVE)
                        for c in range(count)
                    ],
                    axis=0,
                )
            )
        return result

    def absorb(source, p, count, which, scores):
        factor = 1.0 / math.sqrt(TD) if which == 0 else 1.0
        old = soft[p, which : which + 1, :]
        new = jnp.maximum(old, jnp.max(scores, axis=0, keepdims=True))
        weights = jnp.exp((scores - new) * factor)
        shrink = jnp.exp((old - new) * factor)
        soft[p, which : which + 1, :] = new
        soft[p, which + 2 : which + 3, :] = soft[
            p, which + 2 : which + 3, :
        ] * shrink + jnp.sum(weights, axis=0, keepdims=True)
        rounded = weights.astype(jnp.bfloat16)
        if which == 0:
            values = jnp.concatenate(
                [kv[source, c, rows : 2 * rows, :] for c in range(count)], axis=1
            )
            t_acc[p] = t_acc[p] * shrink + jnp.dot(
                values, rounded, preferred_element_type=jnp.float32
            )
        else:
            key_rows = kv[source, 0:count, 2 * rows : 3 * rows, :].reshape(count * rows, TD)
            s_acc[p] = s_acc[p] * shrink + columns_dot(key_rows, rounded)[TD - SD :]

    def attend(source, pairs, own_place=False):
        scores = masked_scores(source, *pairs[0], own_place)
        for i, (p, count) in enumerate(pairs):
            later = None
            if i + 1 < len(pairs):
                later = masked_scores(source, *pairs[i + 1], own_place)
            for which in range(2):
                absorb(source, p, count, which, scores[which])
            scores = later

    for load in loads[5:]:
        load.wait()
    blank = jnp.zeros((rows, TD - SD), jnp.bfloat16)
    scale = jnp.asarray(1.0 / math.sqrt(SD), jnp.bfloat16)

    def own_turn(r, carry):
        place = partner(r)

        @pl.when(r > 0)
        def _():
            q_copy(r, 0).wait_recv()
            q_copy(r, 1).wait_recv()

        for j in range(heads):
            tq_all[place, j * rows : (j + 1) * rows, :] = tq_in[place, :, j * TD : (j + 1) * TD]
            sq_all[place, j * rows : (j + 1) * rows, :] = jnp.concatenate(
                [sq_in[place, :, j * SD : (j + 1) * SD] * scale, blank], axis=1
            )
        for p in range(npb):

            @pl.when(place == p)
            def _():
                attend(z, [(p, p + 1)], True)

        next_hop(1, place)
        return carry

    lax.fori_loop(0, npb, own_turn, 0)

    def hops(h, early, pieces):
        for c in pieces:

            @pl.when(((h >= 2) & (h <= nkv - 2)) if early else (h == nkv - 1))
            def _():
                next_hop(h, c)

    def turn(h, carry):
        hops(h + 1, True, range(1))
        hops(h, False, range(npb - 1))

        @pl.when(z - h >= 0)
        def _():
            attend(z - h, [(p, p + 1) for p in range(npb - 1)])

        hops(h + 1, True, range(1, npb - 1))
        hops(h, False, range(npb - 1, npb))

        @pl.when(z - h >= 0)
        def _():
            attend(z - h, [(npb - 1, npb)])

        hops(h + 1, True, range(npb - 1, npb))

        @pl.when(z + h <= nkv - 1)
        def _():
            attend(z + h, [(p, p) for p in range(1, npb)])

        return carry

    lax.fori_loop(1, nkv, turn, 0)

    def by_token(row):
        total = row[:, 0:rows]
        for j in range(1, heads):
            total = total + row[:, j * rows : (j + 1) * rows]
        return total

    t_sums, s_sums, t_outs, s_outs = [], [], [], []
    for p in range(npb):
        t_out = (t_acc[p] / soft[p, 2:3, :]).astype(jnp.bfloat16).astype(jnp.float32)
        s_out = (s_acc[p] / soft[p, 3:4, :]).astype(jnp.bfloat16).astype(jnp.float32)
        t_acc[p] = t_out
        s_acc[p] = s_out
        t_sums.append(by_token(jnp.sum(t_out * t_out, axis=0, keepdims=True)))
        s_sums.append(by_token(jnp.sum(s_out * s_out, axis=0, keepdims=True)))

    plane = npb * nha
    slot = pb * nha + ha

    def share(buffer, send, recv, r):
        to = (slot + r) % plane
        return pltpu.make_async_remote_copy(
            src_ref=buffer.at[slot],
            dst_ref=buffer.at[slot],
            send_sem=send.at[r],
            recv_sem=recv.at[r],
            device_id=(to // nha, z, to % nha),
            device_id_type=MESH,
        )

    stats[slot] = jnp.concatenate(t_sums + s_sums, axis=0)
    for r in range(1, plane):
        share(stats, stat_send, stat_recv, r).start()
    for r in range(1, plane):
        share(stats, stat_send, stat_recv, r).wait_recv()
    sums = stats[0]
    for i in range(1, plane):
        sums = sums + stats[i]
    t_scale = lax.rsqrt(sums[0:npb] * (1.0 / (heads * plane * TD)) + EPSILON)
    s_scale = lax.rsqrt(sums[npb : 2 * npb] * (1.0 / (heads * plane * SD)) + EPSILON)

    loss = jnp.zeros((1, npb * rows), jnp.float32)
    features, differences = [], []
    for j in range(heads):
        cut = slice(j * rows, (j + 1) * rows)
        target = jnp.concatenate(
            [t_acc[p, :, cut] * t_scale[p : p + 1] for p in range(npb)], axis=1
        )
        feature = jnp.concatenate(
            [s_acc[p, :, cut] * s_scale[p : p + 1] for p in range(npb)], axis=1
        ).astype(jnp.bfloat16)
        difference = columns_dot(w_ref[j], feature) - target
        loss = loss + jnp.sum(difference * difference, axis=0, keepdims=True)
        features.append(feature)
        differences.append(difference)
    losses[slot] = jnp.concatenate(
        [loss[:, p * rows : (p + 1) * rows] for p in range(npb)]
        + [jnp.zeros((8 - npb, rows), jnp.float32)],
        axis=0,
    )
    for r in range(1, plane):
        share(losses, loss_send, loss_recv, r).start()

    def grad_copy(j):
        return pltpu.make_async_remote_copy(
            src_ref=grads.at[j],
            dst_ref=grads_in.at[z],
            send_sem=grad_send.at[j],
            recv_sem=grad_recv.at[z],
            device_id=coords(first_head + j),
            device_id_type=MESH,
        )

    for j in range(heads):
        high = differences[j].astype(jnp.bfloat16)
        low = (differences[j] - high.astype(jnp.float32)).astype(jnp.bfloat16)
        grads[j] = rows_dot(features[j], high) + rows_dot(features[j], low)

        @pl.when(first_head + j != me)
        def _():
            grad_copy(j).start()

        @pl.when(first_head + j == me)
        def _():
            grads_in[z] = grads[j]

    for r in range(1, plane):
        share(losses, loss_send, loss_recv, r).wait_recv()
    mine = losses[0, pl.ds(pb, 1), :]
    for i in range(1, plane):
        mine = mine + losses[i, pl.ds(pb, 1), :]
    part = rows // nha
    chosen = mine[:, 0:part]
    for i in range(1, nha):
        chosen = jnp.where(ha == i, mine[:, i * part : (i + 1) * part], chosen)
    loss_ref[...] = chosen * (1.0 / (heads * plane * TD))

    giver_ha = me // (npb * heads)
    giver_pb = (me // heads) % npb
    for i in range(nkv):

        @pl.when((giver_ha != ha) | (giver_pb != pb) | (z != i))
        def _():
            pltpu.make_async_remote_copy(
                src_ref=grads.at[0],
                dst_ref=grads_in.at[i],
                send_sem=grad_send.at[0],
                recv_sem=grad_recv.at[i],
                device_id=(giver_pb, i, giver_ha),
                device_id_type=MESH,
            ).wait_recv()

    total = grads_in[0]
    for i in range(1, nkv):
        total = total + grads_in[i]
    grad_ref[...] = total * (1.0 / math.sqrt(tokens))

    for r in range(1, npb):
        kv_copy(r).wait_send()
        q_copy(r, 0).wait_send()
        q_copy(r, 1).wait_send()
    for h in range(nkv - 1):
        for c in range(npb):

            @pl.when((z - h >= 0) & (z < nkv - 1))
            def _():
                chain(h, c, True).wait_send()

            if c < npb - 1:

                @pl.when((z + h <= nkv - 1) & (z > 0))
                def _():
                    chain(h, c, False).wait_send()

    for r in range(1, plane):
        share(stats, stat_send, stat_recv, r).wait_send()
        share(losses, loss_send, loss_recv, r).wait_send()
    for j in range(heads):

        @pl.when(first_head + j != me)
        def _():
            grad_copy(j).wait_send()


def by_heads(
    shape, teacher_q, teacher_k, teacher_v, student_q, student_k, student_v, doc_ids, proj_weight
):
    npb, nkv, nha = shape
    rows = teacher_q.shape[0]
    heads = teacher_q.shape[1] // (npb * TD)
    wide = heads * rows
    plane = npb * nha
    dma = pltpu.SemaphoreType.DMA
    bf16, f32 = jnp.bfloat16, jnp.float32
    vmem = pl.BlockSpec(memory_space=pltpu.VMEM)
    grad, loss = pl.pallas_call(
        functools.partial(fused, shape, rows * npb * nkv),
        out_shape=(
            jax.ShapeDtypeStruct((SD, TD), f32),
            jax.ShapeDtypeStruct((1, rows // nha), f32),
        ),
        in_specs=[pl.BlockSpec(memory_space=pltpu.HBM)] * 8,
        out_specs=(vmem, vmem),
        scratch_shapes=[
            pltpu.VMEM(teacher_k.shape, bf16),
            pltpu.VMEM(teacher_v.shape, bf16),
            pltpu.VMEM(student_k.shape, bf16),
            pltpu.VMEM(student_v.shape, bf16),
            pltpu.VMEM((1, rows), jnp.int32),
            pltpu.VMEM((heads, SD, TD), bf16),
            pltpu.VMEM((npb, 3 * rows + 16, TD), bf16),
            pltpu.VMEM((nkv, npb, 3 * rows + 16, TD), bf16),
            pltpu.VMEM((npb, rows, heads * TD), bf16),
            pltpu.VMEM((npb, rows, heads * SD), bf16),
            pltpu.VMEM((npb, wide, TD), bf16),
            pltpu.VMEM((npb, wide, TD), bf16),
            pltpu.VMEM((npb, TD, wide), f32),
            pltpu.VMEM((npb, SD, wide), f32),
            pltpu.VMEM((npb, 8, wide), f32),
            pltpu.VMEM((plane, 8, rows), f32),
            pltpu.VMEM((plane, 8, rows), f32),
            pltpu.VMEM((heads, SD, TD), f32),
            pltpu.VMEM((nkv, SD, TD), f32),
            dma((npb,)),
            dma((npb,)),
            dma((npb, 2)),
            dma((npb, 2)),
            dma((nkv, npb)),
            dma((nkv, npb)),
            dma((nkv, npb)),
            dma((nkv, npb)),
            dma((plane,)),
            dma((plane,)),
            dma((plane,)),
            dma((plane,)),
            dma((heads,)),
            dma((nkv,)),
            dma((8,)),
        ],
        compiler_params=pltpu.CompilerParams(
            collective_id=0, has_side_effects=True, vmem_limit_bytes=63 * 1024 * 1024
        ),
        name="attention_distillation",
    )(
        teacher_q,
        teacher_k,
        teacher_v,
        student_q,
        student_k,
        student_v,
        doc_ids.reshape(1, rows),
        proj_weight,
    )
    return grad, loss.reshape(-1)


def local(*arguments):
    teacher_q, teacher_k, proj_weight = arguments[0], arguments[1], arguments[7]
    shape = tuple(lax.axis_size(name) for name in ("pb", "kv", "ha"))
    groups = teacher_k.shape[1] // TD
    fits = (
        groups == shape[0] == 4
        and shape[2] == 2
        and math.prod(shape) == proj_weight.shape[0]
        and teacher_q.shape[0] == 128
    )
    if fits:
        return by_heads(shape, *arguments)
    return gathered(*arguments)


def solution(mesh):
    in_specs = (
        P(("pb", "kv"), "ha"),
        P(("pb", "kv"), "ha"),
        P(("pb", "kv"), "ha"),
        P(("pb", "kv"), "ha"),
        P(("pb", "kv"), "ha"),
        P(("pb", "kv"), "ha"),
        P(("pb", "kv")),
        P(),
    )
    out_specs = (P(("pb", "kv", "ha"), None), P(("pb", "kv", "ha")))
    return jax.shard_map(local, mesh=mesh, in_specs=in_specs, out_specs=out_specs, check_vma=False)
```
